256 devices in a mesh: outer: 8 (over x, y_hi), inner: 32 (over y_lo, z, core).
Axes of the slice: x: 4, y: 4 (y_hi: 2, y_lo: 2; y = y_hi * 2 + y_lo), z: 8, core: 2. Of those that a mesh axis runs over, the one named last changes fastest.
Arguments:
- query: bfloat16 [2, 16384, 640], P(None, ('outer', 'inner')), may hold values from -16 to 16
- key: bfloat16 [2, 16384, 128], P(None, ('outer', 'inner')), may hold values from -8 to 8
- value: bfloat16 [2, 16384, 128], P(None, ('outer', 'inner')), may hold values from -6 to 6
- d_attended: bfloat16 [2, 16384, 640], P(None, ('outer', 'inner')), may hold values from -6 to 6
- stretch_ids: int32 [256], replicated, may hold values from 0 to 255, each once
Outputs:
- attended: bfloat16 [2, 16384, 640], P(None, ('outer', 'inner'))
- grad_query: float32 [2, 16384, 640], P(None, ('outer', 'inner'))
- grad_key: float32 [2, 16384, 128], P(None, ('outer', 'inner'))
- grad_value: float32 [2, 16384, 128], P(None, ('outer', 'inner'))
The draws below stay inside these ranges and needn't reach their ends.
Inputs may be any that keep to these rules, and one draw needn't show every extreme that they name: `stretch_ids`: each shard number appears once.
All inputs are finite; a program needn't handle non-finite values.
Results may differ from the reference program's by a relative error of at most 0.029.
Values may be sent and summed in bfloat16 or wider, within the bound.
No kernel may reach another device: no remote copies, remote signals or barrier semaphores. Data moves between devices by JAX's collectives and lax.ppermute only.
A program may use at most 128 MiB of HBM per device.

```python
import math
import jax
import jax.numpy as jnp
from jax import lax

HEADS = 5
HEAD_DIM = 128
TOK_DEV = 64
SEQS = 2
STRETCH = 32
SHARDS = 256
LENGTH = 16384


def draw_query(key, part):
    key = jax.random.fold_in(key, 11)
    extent = (SEQS, LENGTH, HEADS * HEAD_DIM)
    values = jnp.clip(jax.random.normal(key, extent, jnp.float32) * 2.5, -16.0, 16.0)
    return values.astype(jnp.bfloat16)


def draw_key(key, part):
    key = jax.random.fold_in(key, 12)
    extent = (SEQS, LENGTH, HEAD_DIM)
    values = jnp.clip(jax.random.normal(key, extent, jnp.float32), -8.0, 8.0)
    return values.astype(jnp.bfloat16)


def block_levels(key, shape, cuts, smallest, top_value):
    level, own = 1.0, jax.random.fold_in(key, 6)
    for dim, shards_of in cuts:
        steps = jnp.exp(jax.random.uniform(jax.random.fold_in(own, dim), (shards_of,), jnp.float32, smallest / len(cuts), top_value / len(cuts)))
        level = level * jnp.repeat(steps, shape[dim] // shards_of).reshape([-1 if axis == dim else 1 for axis in range(len(shape))])
    return level


def centred(key, shape, scale, reach, split=(), held_as=jnp.bfloat16):
    result = scale * jax.random.normal(key, shape, jnp.float32)
    if split:
        result = result * block_levels(key, shape, split, -0.22, 0.18)
    return jnp.clip(result, -reach, reach).astype(held_as)


def setup_inputs(seed: int = 0) -> dict:
    seeds = jax.random.split(jax.random.key(seed), 6)
    return {
        "query": draw_query(jax.random.fold_in(seeds[5], 71), 0),
        "key": draw_key(jax.random.fold_in(seeds[5], 71), 0),
        "value": centred(seeds[2], (SEQS, LENGTH, HEAD_DIM), 1.0, 6.0, ((1, 256),)),
        "d_attended": centred(seeds[3], (SEQS, LENGTH, HEADS * HEAD_DIM), 1.0, 6.0, ((1, 256),)),
        "stretch_ids": jax.random.permutation(seeds[4], SHARDS).astype(jnp.int32),
    }


def token_positions(stretch_ids):
    row_index = jnp.arange(LENGTH, dtype=jnp.int32)
    shard_of = row_index // TOK_DEV
    offset = row_index % TOK_DEV
    stretch_of = stretch_ids[shard_of].astype(jnp.int32)
    leading = stretch_of * STRETCH + offset
    trailing = (2 * SHARDS - 1 - stretch_of) * STRETCH + offset - STRETCH
    return jnp.where(offset < STRETCH, leading, trailing)


def one_sequence(query, key, value, d_attended, positions):
    block_rows = math.gcd(LENGTH, 512)
    block_count = LENGTH // block_rows
    scaling = HEAD_DIM ** -0.5
    query_blocks = query.reshape(block_count, block_rows * HEADS, HEAD_DIM)
    grad_blocks = d_attended.reshape(block_count, block_rows * HEADS, HEAD_DIM)
    place_blocks = jnp.repeat(positions, HEADS).reshape(block_count, block_rows * HEADS)
    value_wide = value.astype(jnp.float32)

    def score_block(query_rows, row_places):
        scores = jnp.dot(query_rows, key.T, preferred_element_type=jnp.float32) * scaling
        visible = positions[None, :] <= row_places[:, None]
        return scores, visible

    def forward(inputs):
        query_rows, row_places = inputs
        scores, visible = score_block(query_rows, row_places)
        row_max = jnp.max(jnp.where(visible, scores, -jnp.inf), axis=1)
        weights = jnp.where(visible, jnp.exp(scores - row_max[:, None]), 0.0)
        row_sum = jnp.sum(weights, axis=1)
        mixed = jnp.dot(weights, value_wide, precision=lax.Precision.HIGHEST, preferred_element_type=jnp.float32)
        return (mixed / row_sum[:, None]).astype(jnp.bfloat16), row_max + jnp.log(row_sum)

    attended_blocks, log_sums = lax.map(forward, (query_blocks, place_blocks))

    def backward(running, inputs):
        grad_key, grad_value = running
        query_rows, row_places, grad_rows, attended_rows, log_rows = inputs
        scores, visible = score_block(query_rows, row_places)
        attention = jnp.where(visible, jnp.exp(scores - log_rows[:, None]), 0.0)
        row_delta = jnp.sum(grad_rows.astype(jnp.float32) * attended_rows.astype(jnp.float32), axis=1)
        grad_weights = jnp.dot(grad_rows, value.T, preferred_element_type=jnp.float32)
        grad_scores = (attention * (grad_weights - row_delta[:, None])).astype(jnp.bfloat16)
        grad_query = jnp.dot(grad_scores, key, preferred_element_type=jnp.float32) * scaling
        grad_key = grad_key + jnp.dot(grad_scores.T, query_rows, preferred_element_type=jnp.float32) * scaling
        grad_value = grad_value + jnp.dot(attention.astype(jnp.bfloat16).T, grad_rows, preferred_element_type=jnp.float32)
        return (grad_key, grad_value), grad_query

    empty_grad = jnp.zeros((LENGTH, HEAD_DIM), jnp.float32)
    (grad_key, grad_value), grad_query = lax.scan(backward, (empty_grad, empty_grad), (query_blocks, place_blocks, grad_blocks, attended_blocks, log_sums))
    attended = attended_blocks.reshape(LENGTH, HEADS * HEAD_DIM)
    return attended, grad_query.reshape(LENGTH, HEADS * HEAD_DIM), grad_key, grad_value


def reference(query, key, value, d_attended, stretch_ids):
    positions = token_positions(stretch_ids)
    results = [one_sequence(query[sequence], key[sequence], value[sequence], d_attended[sequence], positions) for sequence in range(SEQS)]
    attended = jnp.stack([entry[0] for entry in results], axis=0)
    grad_query = jnp.stack([entry[1] for entry in results], axis=0)
    grad_key = jnp.stack([entry[2] for entry in results], axis=0)
    grad_value = jnp.stack([entry[3] for entry in results], axis=0)
    return (attended, grad_query, grad_key, grad_value)
```

```python
import functools, math
import jax
import jax.numpy as jnp
from jax import lax
from jax.experimental import pallas as pl
from jax.experimental.pallas import tpu as pltpu
from jax.sharding import PartitionSpec as P

bf16, f32, i32 = jnp.bfloat16, jnp.float32, jnp.int32
HIDE = -float(2**18)
NONE = -1e30
NT = (((1,), (1,)), ((), ()))
NN = (((1,), (0,)), ((), ()))
SMEM = pl.BlockSpec(memory_space=pltpu.SMEM)
VMEM = pl.BlockSpec(memory_space=pltpu.VMEM)
LIMIT = 48 * 2**20
AXES = ("outer", "inner")
NX, NY, NZ = 4, 4, 8


def dot(a, b, dims=NN):
    return lax.dot_general(a, b, dims, preferred_element_type=f32)


class Cfg:
    def __init__(s, heads, half, width, C=512, R=256):
        s.heads, s.half, s.width, s.C, s.R = heads, half, width, C, R
        s.tokens = 4 * half
        s.row_blocks, s.key_blocks = 4 * NX, 4 * NY * NZ
        s.span = half * heads
        s.rows, s.keys = s.row_blocks * s.span, s.key_blocks * half
        s.nr, s.nc = s.rows // R, s.keys // C
        s.slab = s.keys // NY


def place(x, y, z, core):
    return (x * 2 + (y >> 1)) * 32 + ((y & 1) * NZ + z) * 2 + core


def shift(a, dx=0, dy=0, dz=0, core=0):
    pairs = [(place(x, y, z, c), place((x + dx) % NX, (y + dy) % NY, (z + dz) % NZ, c ^ core))
             for x in range(NX) for y in range(NY) for z in range(NZ) for c in range(2)]
    return lax.ppermute(a, AXES, pairs)


def tables_body(cfg, shard_count, ids, tab_ref, qpos_ref):
    hf, span = cfg.half, cfg.span
    outer_at, inner_at = lax.axis_index("outer"), lax.axis_index("inner")
    x, core = outer_at >> 1, inner_at & 1
    y, z = (outer_at & 1) * 2 + (inner_at >> 4), (inner_at >> 1) & 7
    top = 2 * shard_count - 1
    line = lax.broadcasted_iota(i32, (1, 128), 1)

    def ranked(count, source):
        held = jnp.full((1, 128), 0, i32)
        for j in range(count):
            held = jnp.where(line >> 1 == j, ids[source(j)], held)
        held = jnp.where(line & 1 == 1, top - held, held)
        held = jnp.where(line < 2 * count, held, top + 1 + line).astype(f32)
        across = jnp.broadcast_to(held, (128, 128))
        down = across.T
        lane = lax.broadcasted_iota(i32, (128, 128), 1)
        rank = jnp.sum((down < across).astype(f32), axis=0, keepdims=True)
        rank_down = jnp.sum((across < down).astype(f32), axis=1, keepdims=True).astype(i32)
        rising = jnp.sum(jnp.where(rank_down == lane, down, 0.0), axis=0, keepdims=True)
        return rank, rising

    row_rank, rows = ranked(2 * NX, lambda j: place((x + (j >> 1)) & (NX - 1), y, z, core ^ (j & 1)))
    key_rank, keys = ranked(2 * NY * NZ, lambda j: place(x, (y + (j >> 4)) & (NY - 1), (z + ((j >> 1) & 7)) & (NZ - 1), core ^ (j & 1)))
    row_down = jnp.broadcast_to(rows, (128, 128)).T
    counts = jnp.zeros((1, 128), f32)
    for r in range(cfg.nr):
        first, last = r * cfg.R // span, ((r + 1) * cfg.R - 1) // span
        seen = jnp.sum((keys <= row_down[last:last + 1]).astype(f32), axis=1, keepdims=True)
        whole = jnp.sum((keys < row_down[first:first + 1]).astype(f32), axis=1, keepdims=True)
        counts = jnp.where(line == r, jnp.floor((seen * hf + (cfg.C - 1)) * (1.0 / cfg.C)), counts)
        counts = jnp.where(line == 64 + r, jnp.floor(whole * hf * (1.0 / cfg.C)), counts)
    tab_ref[0:1] = row_rank.astype(i32)
    tab_ref[1:2] = key_rank.astype(i32)
    tab_ref[2:3] = keys.astype(i32)
    tab_ref[3:4] = counts.astype(i32)
    spot = lax.broadcasted_iota(i32, (1, cfg.rows), 1)
    pos = jnp.zeros((1, cfg.rows), f32)
    for i in range(cfg.row_blocks):
        pos = jnp.where(spot >= i * span, row_down[i:i + 1, :1], pos)
    qpos_ref[...] = pos.astype(i32) * hf + (spot & (hf - 1))


def tables(cfg, ids):
    return pl.pallas_call(
        functools.partial(tables_body, cfg, ids.shape[0]),
        out_shape=(jax.ShapeDtypeStruct((4, 128), i32), jax.ShapeDtypeStruct((1, cfg.rows), i32)),
        in_specs=[SMEM], out_specs=(VMEM,) * 2, name="tables",
    )(ids)


def aligned(at, by):
    return at * by if isinstance(at, int) else pl.multiple_of(at * by, by)


def load_rows(cfg, tab, sources, dst):
    w, hf, hd = cfg.width, cfg.half, cfg.heads
    for i in range(cfg.row_blocks):
        at = aligned(tab[0, i], cfg.span)
        for h in range(hd):
            dst[pl.ds(pl.multiple_of(at + h * hf, hf), hf), :] = sources[i // 4][(i % 4) * hf:(i % 4 + 1) * hf, h * w:(h + 1) * w]


def load_keys(cfg, tab, sources, ks, vs):
    w, hf = cfg.width, cfg.half
    per = cfg.key_blocks // len(sources)
    for n, source in enumerate(sources):
        def step(j, _):
            to = pl.ds(aligned(tab[1, n * per + j], hf), hf)
            block = source[pl.ds(aligned(j, hf), hf), :]
            ks[to, :] = block[:, :w]
            vs[to, :] = block[:, w:]
            return 0

        lax.fori_loop(0, per, step, 0, unroll=4)


def unload_rows(cfg, tab, src, outs):
    w, hf, hd = cfg.width, cfg.half, cfg.heads
    for i in range(cfg.row_blocks):
        at = aligned(tab[0, i], cfg.span)
        for h in range(hd):
            outs[i // 4][(i % 4) * hf:(i % 4 + 1) * hf, h * w:(h + 1) * w] = src[pl.ds(pl.multiple_of(at + h * hf, hf), hf), :].astype(bf16)


def visible(cfg, tab, qpos_ref, c, r):
    hf, C, R = cfg.half, cfg.C, cfg.R
    per = C // hf
    step = lax.broadcasted_iota(i32, (hf, 128), 0)
    held = jnp.concatenate([step + tab[2, c * per + b] * hf for b in range(per)], axis=0)
    wide = jnp.concatenate([held] * (R // 128), axis=1)
    return wide <= qpos_ref[:, pl.ds(aligned(r, R), R)]


def forward_body(cfg, *refs):
    tab, qpos = refs[:2]
    q, kv, do = refs[2:6], refs[6:10], refs[10:14]
    outs, stat_ref = refs[14:18], refs[18]
    qs, ks, vs, vt, dos, os, ls = refs[19:]
    w, C, R = cfg.width, cfg.C, cfg.R
    load_rows(cfg, tab, q, qs)
    load_rows(cfg, tab, do, dos)
    load_keys(cfg, tab, kv, ks, vs)
    for c in range(cfg.keys // 256):
        vt[:, c * 256:(c + 1) * 256] = vs[c * 256:(c + 1) * 256, :].T
    scale = math.log2(math.e) / math.sqrt(w)

    def tile(r, _):
        here = pl.ds(aligned(r, R), R)

        def step(masked, c, state):
            m, l, acc = state
            keys = pl.ds(aligned(c, C), C)
            s = dot(ks[keys, :], qs[here, :], NT)
            if masked:
                s = jnp.where(visible(cfg, tab, qpos, c, r), s, HIDE)
            top = jnp.maximum(m, jnp.max(s, axis=0, keepdims=True) * scale)
            p = jnp.exp2(s * scale - top)
            shrink = jnp.exp2(m - top)
            l = l * shrink + jnp.sum(p, axis=0, keepdims=True)
            acc = acc * shrink + dot(vt[:, keys], p.astype(bf16))
            return top, l, acc

        state = (jnp.full((1, R), NONE, f32), jnp.zeros((1, R), f32), jnp.zeros((w, R), f32))
        state = lax.fori_loop(0, tab[3, 64 + r], functools.partial(step, False), state)
        m, l, acc = lax.fori_loop(tab[3, 64 + r], tab[3, r], functools.partial(step, True), state)
        safe = jnp.maximum(l, 1e-30)
        acc = acc * (1.0 / safe)
        lse = m + jnp.log2(safe)
        stat_ref[0:1, here] = lse
        stat_ref[1:2, here] = jnp.sum(acc * dos[here, :].astype(f32).T, axis=0, keepdims=True)
        os[here, :] = acc.T
        ls[here, :] = jnp.broadcast_to(lse, (w, R)).T
        return 0

    lax.fori_loop(0, cfg.nr, tile, 0)
    unload_rows(cfg, tab, os, outs)
    hf, hd = cfg.half, cfg.heads
    lane = lax.broadcasted_iota(i32, (hf, w), 1)
    for i in range(cfg.row_blocks):
        at = aligned(tab[0, i], cfg.span)
        extra = jnp.zeros((hf, w), f32)
        for h in range(hd):
            rest = ls[pl.ds(pl.multiple_of(at + h * hf, hf), hf), :]
            for n in range(3):
                piece = rest.astype(bf16).astype(f32)
                extra = jnp.where(lane == 3 * h + n, piece, extra)
                rest = rest - piece
        outs[i // 4][(i % 4) * hf:(i % 4 + 1) * hf, hd * w:] = extra.astype(bf16)


def forward(cfg, tab, qpos, q, kv, do):
    wide = cfg.heads * cfg.width
    row, key = (cfg.rows, cfg.width), (cfg.keys, cfg.width)
    found = pl.pallas_call(
        functools.partial(forward_body, cfg),
        out_shape=(jax.ShapeDtypeStruct((cfg.tokens, wide + cfg.width), bf16),) * 4 + (jax.ShapeDtypeStruct((2, cfg.rows), f32),),
        in_specs=[SMEM] + [VMEM] * 13, out_specs=(VMEM,) * 5,
        scratch_shapes=[pltpu.VMEM(row, bf16), pltpu.VMEM(key, bf16), pltpu.VMEM(key, bf16), pltpu.VMEM(key[::-1], bf16),
                        pltpu.VMEM(row, bf16), pltpu.VMEM(row, f32), pltpu.VMEM(row, f32)],
        compiler_params=pltpu.CompilerParams(vmem_limit_bytes=LIMIT),
        name="attend",
    )(tab, qpos, *q, *kv, *do)
    return found[:4], found[4]


def backward_body(cfg, *refs):
    tab, qpos = refs[:2]
    q, kv, do, stat = refs[2:6], refs[6:10], refs[10:14], refs[14:18]
    gq, gkv = refs[18:22], refs[22:26]
    qs, ks, vs, kt, dos, gqs, gks, gvs = refs[26:]
    w, C, R, hf = cfg.width, cfg.C, cfg.R, cfg.half
    load_rows(cfg, tab, q, qs)
    load_rows(cfg, tab, do, dos)
    load_keys(cfg, tab, kv, ks, vs)
    for c in range(cfg.keys // 256):
        kt[:, c * 256:(c + 1) * 256] = ks[c * 256:(c + 1) * 256, :].T
    gks[...] = jnp.zeros_like(gks)
    gvs[...] = jnp.zeros_like(gvs)
    scale = math.log2(math.e) / math.sqrt(w)

    def tile(r, _):
        here = pl.ds(aligned(r, R), R)
        part = [s[0:1, here] for s in stat]
        top = functools.reduce(jnp.maximum, part)
        share = [jnp.exp2(v - top) for v in part]
        total = sum(share)
        lse = top + jnp.log2(total)
        delta = sum(v * s[1:2, here] for v, s in zip(share, stat)) / total

        def step(masked, c, acc):
            keys = pl.ds(aligned(c, C), C)
            s = dot(ks[keys, :], qs[here, :], NT)
            if masked:
                s = jnp.where(visible(cfg, tab, qpos, c, r), s, HIDE)
            p = jnp.exp2(s * scale - lse)
            gw = dot(vs[keys, :], dos[here, :], NT)
            ds = (p * (gw - delta)).astype(bf16)
            gvs[keys, :] += dot(p.astype(bf16), dos[here, :])
            gks[keys, :] += dot(ds, qs[here, :])
            return acc + dot(kt[:, keys], ds)

        acc = lax.fori_loop(0, tab[3, 64 + r], functools.partial(step, False), jnp.zeros((w, R), f32))
        acc = lax.fori_loop(tab[3, 64 + r], tab[3, r], functools.partial(step, True), acc)
        gqs[here, :] = acc.T
        return 0

    lax.fori_loop(0, cfg.nr, tile, 0)
    unload_rows(cfg, tab, gqs, gq)
    per = cfg.key_blocks // len(gkv)
    for n, out in enumerate(gkv):
        def put(j, _):
            own = pl.ds(aligned(tab[1, n * per + j], hf), hf)
            to = pl.ds(aligned(j, hf), hf)
            out[to, :w] = gks[own, :].astype(bf16)
            out[to, w:] = gvs[own, :].astype(bf16)
            return 0

        lax.fori_loop(0, per, put, 0, unroll=4)


def backward(cfg, tab, qpos, q, kv, do, stat):
    row, key = (cfg.rows, cfg.width), (cfg.keys, cfg.width)
    found = pl.pallas_call(
        functools.partial(backward_body, cfg),
        out_shape=(jax.ShapeDtypeStruct((cfg.tokens, cfg.heads * cfg.width), bf16),) * 4
        + (jax.ShapeDtypeStruct((cfg.slab, 2 * cfg.width), bf16),) * 4,
        in_specs=[SMEM] + [VMEM] * 17, out_specs=(VMEM,) * 8,
        scratch_shapes=[pltpu.VMEM(row, bf16), pltpu.VMEM(key, bf16), pltpu.VMEM(key, bf16), pltpu.VMEM(key[::-1], bf16),
                        pltpu.VMEM(row, bf16), pltpu.VMEM(row, f32), pltpu.VMEM(key, f32), pltpu.VMEM(key, f32)],
        compiler_params=pltpu.CompilerParams(vmem_limit_bytes=LIMIT),
        name="grads",
    )(tab, qpos, *q, *kv, *do, *stat)
    return found[:4], found[4:]


def merge_body(cfg, *refs):
    parts, outs = refs[:4], refs[4:]
    w, hd, n = cfg.width, cfg.heads, cfg.tokens // 2
    extra = [p[:, hd * w:].astype(f32) for p in parts]
    level = [e + pltpu.roll(e, w - 1, 1) + pltpu.roll(e, w - 2, 1) for e in extra]
    top = functools.reduce(jnp.maximum, level)
    share = [jnp.exp2(v - top) for v in level]
    total = 1.0 / sum(share)
    share = [v * total for v in share]
    for h in range(hd):
        at = slice(h * w, (h + 1) * w)
        mixed = sum(p[:, at].astype(f32) * v[:, 3 * h:3 * h + 1] for p, v in zip(parts, share)).astype(bf16)
        outs[0][:, at] = mixed[:n]
        outs[1][:, at] = mixed[n:]


def merge(cfg, parts):
    out = jax.ShapeDtypeStruct((cfg.tokens // 2, cfg.heads * cfg.width), bf16)
    return pl.pallas_call(functools.partial(merge_body, cfg), out_shape=(out, out), in_specs=[VMEM] * 4,
                          out_specs=(VMEM,) * 2, name="merge")(*parts)


def add(parts):
    return functools.reduce(jnp.add, [p.astype(f32) for p in parts])


def on_device(query, key, value, d_attended, stretch_ids):
    width = key.shape[2]
    cfg = Cfg(query.shape[2] // width, key.shape[1] // 2, width)
    core = lax.axis_index("inner") & 1
    tab, qpos = tables(cfg, stretch_ids)

    def paired(a):
        mine = lax.dynamic_index_in_dim(a, core, 0, False)
        given = lax.dynamic_index_in_dim(a, 1 - core, 0, False)
        return jnp.concatenate([mine, shift(given, core=1)], axis=0)

    pairs = paired(jnp.concatenate([key, value], axis=2))
    q0 = paired(query)
    do0 = paired(d_attended)
    slab = jnp.concatenate([pairs] + [shift(pairs, dz=-d) for d in range(1, NZ)], axis=0)
    q = [q0] + [shift(q0, dx=-d) for d in range(1, NX)]
    kv = [slab] + [shift(slab, dy=-d) for d in range(1, NY)]
    do = [do0] + [shift(do0, dx=-d) for d in range(1, NX)]
    parts, stat = forward(cfg, tab, qpos, q, kv, do)
    stats = [stat] + [shift(stat, dx=-d) for d in range(1, NX)]
    sent = [parts[0]] + [shift(parts[d], dx=d) for d in range(1, NX)]
    gq, gkv = backward(cfg, tab, qpos, q, kv, do, stats)
    slab = add([gkv[0]] + [shift(gkv[d], dy=d) for d in range(1, NY)]).astype(bf16)
    n = cfg.tokens
    gkv = add([slab[:n]] + [shift(slab[d * n:(d + 1) * n], dz=d) for d in range(1, NZ)])
    gq = add([gq[0]] + [shift(gq[d], dx=d) for d in range(1, NX)])
    att, att_given = merge(cfg, sent)

    def settled(mine, given):
        got = shift(given, core=1)
        return jnp.where(core == 0, jnp.stack([mine, got]), jnp.stack([got, mine]))

    half = n // 2
    scaling = width ** -0.5
    att = settled(att, att_given)
    gq = settled(gq[:half], gq[half:]) * scaling
    gkv = settled(gkv[:half], gkv[half:])
    return att, gq, gkv[..., :width] * scaling, gkv[..., width:]


def solution(mesh):
    split = P(None, AXES, None)
    return jax.shard_map(on_device, mesh=mesh, in_specs=(split,) * 4 + (P(),), out_specs=(split,) * 4, check_vma=False)
```

```python
import functools, math
import jax
import jax.numpy as jnp
from jax import lax
from jax.experimental import pallas as pl
from jax.experimental.pallas import tpu as pltpu
from jax.sharding import PartitionSpec as P

bf16, f32, i32 = jnp.bfloat16, jnp.float32, jnp.int32
HIDE = -float(2**18)
NONE = -1e30
NT = (((1,), (1,)), ((), ()))
NN = (((1,), (0,)), ((), ()))
SMEM = pl.BlockSpec(memory_space=pltpu.SMEM)
VMEM = pl.BlockSpec(memory_space=pltpu.VMEM)
LIMIT = 20 * 2**20
AXES = ("outer", "inner")
NX, NY, NZ = 4, 4, 8


def dot(a, b, dims=NN):
    return lax.dot_general(a, b, dims, preferred_element_type=f32)


class Cfg:
    def __init__(s, heads, half, width, C=256, R=256, G=4):
        s.heads, s.half, s.width, s.C, s.R, s.G = heads, half, width, C, R, G
        s.tokens = 4 * half
        s.span = half * heads
        s.row_blocks, s.slab_blocks = 4 * NX, 4 * NZ
        s.rows, s.slab = s.row_blocks * s.span, s.slab_blocks * half
        s.nr = s.rows // R


def place(x, y, z, core):
    return (x * 2 + (y >> 1)) * 32 + ((y & 1) * NZ + z) * 2 + core


def shift(a, dx=0, dy=0, dz=0, core=0):
    pairs = [(place(x, y, z, c), place((x + dx) % NX, (y + dy) % NY, (z + dz) % NZ, c ^ core))
             for x in range(NX) for y in range(NY) for z in range(NZ) for c in range(2)]
    return lax.ppermute(a, AXES, pairs)


def tables_body(cfg, sets, shard_count, ids, *refs):
    tabs, qpos_ref = refs[:-1], refs[-1]
    hf, span = cfg.half, cfg.span
    outer_at, inner_at = lax.axis_index("outer"), lax.axis_index("inner")
    x, core = outer_at >> 1, inner_at & 1
    y, z = (outer_at & 1) * 2 + (inner_at >> 4), (inner_at >> 1) & 7
    top = 2 * shard_count - 1
    line = lax.broadcasted_iota(i32, (1, 128), 1)

    def ranked(count, source):
        held = jnp.full((1, 128), 0, i32)
        for j in range(count):
            held = jnp.where(line >> 1 == j, ids[source(j)], held)
        held = jnp.where(line & 1 == 1, top - held, held)
        held = jnp.where(line < 2 * count, held, top + 1 + line).astype(f32)
        across = jnp.broadcast_to(held, (128, 128))
        down = across.T
        lane = lax.broadcasted_iota(i32, (128, 128), 1)
        rank = jnp.sum((down < across).astype(f32), axis=0, keepdims=True)
        rank_down = jnp.sum((across < down).astype(f32), axis=1, keepdims=True).astype(i32)
        rising = jnp.sum(jnp.where(rank_down == lane, down, 0.0), axis=0, keepdims=True)
        return rank, rising

    row_rank, rows = ranked(2 * NX, lambda j: place((x + (j >> 1)) & (NX - 1), y, z, core ^ (j & 1)))
    row_down = jnp.broadcast_to(rows, (128, 128)).T
    for slabs, tab_ref in zip(sets, tabs):
        key_rank, keys = ranked(
            2 * NZ * len(slabs), lambda j: place(x, (y + slabs[j >> 4]) & (NY - 1), (z + ((j >> 1) & 7)) & (NZ - 1), core ^ (j & 1)))
        counts = jnp.zeros((1, 128), f32)
        for r in range(cfg.nr):
            last = ((r + 1) * cfg.R - 1) // span
            seen = jnp.sum((keys <= row_down[last:last + 1]).astype(f32), axis=1, keepdims=True)
            chunks = jnp.maximum(jnp.floor((seen * hf + (cfg.C - 1)) * (1.0 / cfg.C)), 1.0)
            counts = jnp.where(line == r, chunks, counts) + jnp.where(line == 127, chunks, 0.0)
        tab_ref[0:1] = row_rank.astype(i32)
        tab_ref[1:2] = key_rank.astype(i32)
        tab_ref[2:3] = keys.astype(i32)
        tab_ref[3:4] = counts.astype(i32)
    spot = lax.broadcasted_iota(i32, (1, cfg.rows), 1)
    pos = jnp.zeros((1, cfg.rows), f32)
    for i in range(cfg.row_blocks):
        pos = jnp.where(spot >= i * span, row_down[i:i + 1, :1], pos)
    qpos_ref[...] = pos.astype(i32) * hf + (spot & (hf - 1))


def tables(cfg, sets, ids):
    found = pl.pallas_call(
        functools.partial(tables_body, cfg, sets, ids.shape[0]),
        out_shape=(jax.ShapeDtypeStruct((4, 128), i32),) * len(sets) + (jax.ShapeDtypeStruct((1, cfg.rows), i32),),
        in_specs=[SMEM], out_specs=(VMEM,) * (len(sets) + 1), name="tables",
    )(ids)
    return found[:-1], found[-1]


def aligned(at, by):
    return at * by if isinstance(at, int) else pl.multiple_of(at * by, by)


def load_rows(cfg, tab, sources, dst, base=0):
    w, hf, hd = cfg.width, cfg.half, cfg.heads
    for i in range(cfg.row_blocks):
        at = aligned(tab[0, i], cfg.span)
        for h in range(hd):
            dst[pl.ds(pl.multiple_of(at + h * hf, hf), hf), :] = sources[i // 4][(i % 4) * hf:(i % 4 + 1) * hf, (base + h) * w:(base + h + 1) * w]


def load_keys(cfg, tab, sources, ks, vs):
    w, hf = cfg.width, cfg.half
    per = cfg.slab_blocks
    for n, source in enumerate(sources):
        def step(j, _):
            to = pl.ds(aligned(tab[1, n * per + j], hf), hf)
            block = source[pl.ds(aligned(j, hf), hf), :]
            ks[to, :] = block[:, :w]
            vs[to, :] = block[:, w:]
            return 0

        lax.fori_loop(0, per, step, 0, unroll=4)


def unload_rows(cfg, tab, src, outs):
    w, hf, hd = cfg.width, cfg.half, cfg.heads
    for i in range(cfg.row_blocks):
        at = aligned(tab[0, i], cfg.span)
        for h in range(hd):
            outs[i // 4][(i % 4) * hf:(i % 4 + 1) * hf, h * w:(h + 1) * w] = src[pl.ds(pl.multiple_of(at + h * hf, hf), hf), :].astype(bf16)


def visible(cfg, tab, qpos_ref, c, r):
    hf, C, R = cfg.half, cfg.C, cfg.R
    per = C // hf
    step = lax.broadcasted_iota(i32, (hf, 128), 0)
    held = jnp.concatenate([step + tab[2, c * per + b] * hf for b in range(per)], axis=0)
    wide = jnp.concatenate([held] * (R // 128), axis=1)
    return wide <= qpos_ref[:, pl.ds(aligned(r, R), R)]


def each_tile(cfg, tab, nc, stages):
    def step(_, at):
        group = []
        for _ in range(cfg.G):
            r, c = at
            past = r >= cfg.nr
            group.append((jnp.where(past, 0, r), jnp.where(past, nc - 1, c)))
            end = c + 1 >= tab[3, jnp.where(past, 0, r)]
            at = (jnp.where(end, r + 1, r), jnp.where(end, 0, c + 1))
        held = [()] * cfg.G
        for stage in stages:
            held = [stage(*spot, *value) for spot, value in zip(group, held)]
        return at

    lax.fori_loop(0, lax.div(tab[3, 127] + (cfg.G - 1), cfg.G), step, (jnp.int32(0), jnp.int32(0)))


def work(cfg, n, products):
    pairs = cfg.rows * n * cfg.slab * 5 // 8
    return pl.CostEstimate(flops=4 * products * cfg.width * pairs, bytes_accessed=4 << 20, transcendentals=pairs)


def forward_body(cfg, n, first, last, *refs):
    refs = list(refs)
    take = lambda k: [refs.pop(0) for _ in range(k)]
    (tab, qpos), q, kv = take(2), take(4 if first else 2), take(n)
    before = [] if first else take(2)
    qs, dos = take(2) if first else q
    (stat_ref,) = take(1) if last else [None]
    ml, acc = take(2)
    ks, vs, vt = take(3)
    w, C, R = cfg.width, cfg.C, cfg.R
    keys = n * cfg.slab
    if first:
        load_rows(cfg, tab, q, qs)
        load_rows(cfg, tab, q, dos, cfg.heads)
    load_keys(cfg, tab, kv, ks, vs)
    for c in range(keys // 256):
        vt[:, c * 256:(c + 1) * 256] = vs[c * 256:(c + 1) * 256, :].T
    if first:
        ml[0:1, :] = jnp.full((1, cfg.rows), NONE, f32)
        ml[1:2, :] = jnp.zeros((1, cfg.rows), f32)
        acc[...] = jnp.zeros_like(acc)
    else:
        ml[...] = before[0][...]
        acc[...] = before[1][...]
    scale = math.log2(math.e) / math.sqrt(w)

    def scores(r, c):
        s = dot(ks[pl.ds(aligned(c, C), C), :], qs[pl.ds(aligned(r, R), R), :], NT)
        return (jnp.where(visible(cfg, tab, qpos, c, r), s, HIDE),)

    def weights(r, c, s):
        top = jnp.max(s, axis=0, keepdims=True) * scale
        p = jnp.exp2(s * scale - top)
        return top, jnp.sum(p, axis=0, keepdims=True), dot(vt[:, pl.ds(aligned(c, C), C)], p.astype(bf16))

    def absorb(r, c, top, total, mixed):
        here = pl.ds(aligned(r, R), R)
        old = ml[0:1, here]
        new = jnp.maximum(old, top)
        kept, added = jnp.exp2(old - new), jnp.exp2(top - new)
        ml[0:1, here] = new
        ml[1:2, here] = ml[1:2, here] * kept + total * added
        acc[:, here] = acc[:, here] * kept + mixed * added
        return ()

    each_tile(cfg, tab, keys // C, (scores, weights, absorb))
    if not last:
        return

    def settle(r, _):
        here = pl.ds(aligned(r, 256), 256)
        safe = jnp.maximum(ml[1:2, here], 1e-30)
        mixed = acc[:, here] * (1.0 / safe)
        acc[:, here] = mixed
        stat_ref[0:1, here] = ml[0:1, here] + jnp.log2(safe)
        stat_ref[1:2, here] = jnp.sum(mixed * dos[here, :].astype(f32).T, axis=0, keepdims=True)
        return 0

    lax.fori_loop(0, cfg.rows // 256, settle, 0, unroll=2)


def parts_body(cfg, tab, stat_ref, acc, *refs):
    outs, (os, ls) = refs[:4], refs[4:]
    w, hf, hd = cfg.width, cfg.half, cfg.heads

    def turn(r, _):
        here = pl.ds(aligned(r, 256), 256)
        os[here, :] = acc[:, here].T
        ls[here, :] = jnp.broadcast_to(stat_ref[0:1, here], (w, 256)).T
        return 0

    lax.fori_loop(0, cfg.rows // 256, turn, 0, unroll=2)
    unload_rows(cfg, tab, os, outs)
    lane = lax.broadcasted_iota(i32, (hf, w), 1)
    for i in range(cfg.row_blocks):
        at = aligned(tab[0, i], cfg.span)
        extra = jnp.zeros((hf, w), f32)
        for h in range(hd):
            rest = ls[pl.ds(pl.multiple_of(at + h * hf, hf), hf), :]
            for k in range(3):
                piece = rest.astype(bf16).astype(f32)
                extra = jnp.where(lane == 3 * h + k, piece, extra)
                rest = rest - piece
        outs[i // 4][(i % 4) * hf:(i % 4 + 1) * hf, hd * w:] = extra.astype(bf16)


def parts(cfg, tab, stat, acc):
    row = (cfg.rows, cfg.width)
    return pl.pallas_call(
        functools.partial(parts_body, cfg), out_shape=(jax.ShapeDtypeStruct((cfg.tokens, (cfg.heads + 1) * cfg.width), bf16),) * 4,
        in_specs=[SMEM, VMEM, VMEM], out_specs=(VMEM,) * 4, scratch_shapes=[pltpu.VMEM(row, f32)] * 2, name="parts",
        cost_estimate=pl.CostEstimate(flops=1 << 20, bytes_accessed=12 << 20, transcendentals=0),
    )(tab, stat, acc)


def forward(cfg, tab, qpos, q, kv, last, before=None):
    first, n, w = before is None, len(kv), cfg.width
    row, key = (cfg.rows, w), (n * cfg.slab, w)
    state = [jax.ShapeDtypeStruct((2, cfg.rows), f32), jax.ShapeDtypeStruct((w, cfg.rows), f32)]
    out = ([jax.ShapeDtypeStruct(row, bf16)] * 2 if first else []) + ([state[0]] if last else []) + state
    scratch = [pltpu.VMEM(key, bf16), pltpu.VMEM(key, bf16), pltpu.VMEM(key[::-1], bf16)]
    given = [tab, qpos, *q, *kv, *(before or ())]
    found = pl.pallas_call(
        functools.partial(forward_body, cfg, n, first, last), out_shape=tuple(out),
        in_specs=[SMEM] + [VMEM] * (len(given) - 1), out_specs=(VMEM,) * len(out), scratch_shapes=scratch,
        compiler_params=pltpu.CompilerParams(vmem_limit_bytes=LIMIT), name="attend", cost_estimate=work(cfg, n, 2),
    )(*given)
    return (found[0], found[2]) if last else found


def backward_body(cfg, n, first, last, *refs):
    refs = list(refs)
    take = lambda k: [refs.pop(0) for _ in range(k)]
    (tab, qpos, qs, dos), kv, stat = take(4), take(n), take(4 if first else 1)
    before = [] if first else take(1)
    parts_in = take(4) if last else []
    gq = take(4) if last else []
    (ld,) = take(1) if first else stat
    gqt = [] if last else take(1)
    gkv = take(n)
    ks, vs, kt, gks, gvs = take(5)
    gqt, gqs = (take(2) if last else (gqt[0], None))
    w, C, R, hf = cfg.width, cfg.C, cfg.R, cfg.half
    keys = n * cfg.slab
    load_keys(cfg, tab, kv, ks, vs)
    for c in range(keys // 256):
        kt[:, c * 256:(c + 1) * 256] = ks[c * 256:(c + 1) * 256, :].T
    gks[...] = jnp.zeros_like(gks)
    gvs[...] = jnp.zeros_like(gvs)
    gqt[...] = jnp.zeros_like(gqt) if first else before[0][...]
    if first:
        part = [s[0:1, :] for s in stat]
        top = functools.reduce(jnp.maximum, part)
        share = [jnp.exp2(v - top) for v in part]
        total = sum(share)
        ld[0:1, :] = top + jnp.log2(total)
        ld[1:2, :] = sum(v * s[1:2, :] for v, s in zip(share, stat)) / total
    scale = math.log2(math.e) / math.sqrt(w)

    def scores(r, c):
        at, here = pl.ds(aligned(c, C), C), pl.ds(aligned(r, R), R)
        s = dot(ks[at, :], qs[here, :], NT)
        gw = dot(vs[at, :], dos[here, :], NT)
        return jnp.where(visible(cfg, tab, qpos, c, r), s, HIDE), gw

    def weights(r, c, s, gw):
        here = pl.ds(aligned(r, R), R)
        p = jnp.exp2(s * scale - ld[0:1, here])
        return p.astype(bf16), (p * (gw - ld[1:2, here])).astype(bf16)

    def products(r, c, p, ds):
        at, here = pl.ds(aligned(c, C), C), pl.ds(aligned(r, R), R)
        return dot(p, dos[here, :]), dot(ds, qs[here, :]), dot(kt[:, at], ds)

    def absorb(r, c, gv, gk, gq):
        at, here = pl.ds(aligned(c, C), C), pl.ds(aligned(r, R), R)
        gvs[at, :] += gv
        gks[at, :] += gk
        gqt[:, here] += gq
        return ()

    each_tile(cfg, tab, keys // C, (scores, weights, products, absorb))
    if last:
        def turn(r, _):
            here = pl.ds(aligned(r, 256), 256)
            gqs[here, :] = gqt[:, here].T
            return 0

        lax.fori_loop(0, cfg.rows // 256, turn, 0, unroll=2)
        unload_rows(cfg, tab, gqs, gq)
        for part, out in zip(parts_in, gq):
            out[:, cfg.heads * w:] = part[...]
    for k, out in enumerate(gkv):
        def put(j, _):
            own = pl.ds(aligned(tab[1, k * cfg.slab_blocks + j], hf), hf)
            to = pl.ds(aligned(j, hf), hf)
            out[to, :w] = gks[own, :].astype(bf16)
            out[to, w:] = gvs[own, :].astype(bf16)
            return 0

        lax.fori_loop(0, cfg.slab_blocks, put, 0, unroll=4)


def backward(cfg, tab, qpos, q, kv, stat, before=None, parts=None):
    first, last, n, w = before is None, parts is not None, len(kv), cfg.width
    row, key = (cfg.rows, w), (n * cfg.slab, w)
    if last:
        out = [jax.ShapeDtypeStruct((cfg.tokens, (2 * cfg.heads + 1) * w), bf16)] * 4
    else:
        out = ([jax.ShapeDtypeStruct((2, cfg.rows), f32)] if first else []) + [jax.ShapeDtypeStruct(row[::-1], f32)]
    out += [jax.ShapeDtypeStruct((cfg.slab, 2 * w), bf16)] * n
    scratch = [pltpu.VMEM(key, bf16), pltpu.VMEM(key, bf16), pltpu.VMEM(key[::-1], bf16), pltpu.VMEM(key, f32), pltpu.VMEM(key, f32)]
    if last:
        scratch += [pltpu.VMEM(row[::-1], f32), pltpu.VMEM(row, f32)]
    given = [tab, qpos, *q, *kv, *stat] + ([] if first else [before]) + list(parts or ())
    found = pl.pallas_call(
        functools.partial(backward_body, cfg, n, first, last), out_shape=tuple(out),
        in_specs=[SMEM] + [VMEM] * (len(given) - 1), out_specs=(VMEM,) * len(out), scratch_shapes=scratch,
        compiler_params=pltpu.CompilerParams(vmem_limit_bytes=LIMIT), name="grads", cost_estimate=work(cfg, n, 5),
    )(*given)
    return (found[:4], found[4]) if last else found


def merge_body(cfg, *refs):
    parts, outs = refs[:4], refs[4:]
    w, hd, n = cfg.width, cfg.heads, cfg.tokens // 2
    scaling = w ** -0.5
    extra = [p[:, 2 * hd * w:].astype(f32) for p in parts]
    level = [e + pltpu.roll(e, w - 1, 1) + pltpu.roll(e, w - 2, 1) for e in extra]
    top = functools.reduce(jnp.maximum, level)
    share = [jnp.exp2(v - top) for v in level]
    total = 1.0 / sum(share)
    share = [v * total for v in share]
    for h in range(hd):
        at, behind = slice(h * w, (h + 1) * w), slice((hd + h) * w, (hd + h + 1) * w)
        mixed = sum(p[:, behind].astype(f32) * v[:, 3 * h:3 * h + 1] for p, v in zip(parts, share)).astype(bf16)
        outs[0][:, at] = mixed[:n]
        outs[1][:, at] = mixed[n:]
        summed = sum(p[:, at].astype(f32) for p in parts) * scaling
        outs[2][:, at] = summed[:n]
        outs[3][:, at] = summed[n:]


def merge(cfg, parts):
    out = [jax.ShapeDtypeStruct((cfg.tokens // 2, cfg.heads * cfg.width), t) for t in (bf16, bf16, f32, f32)]
    return pl.pallas_call(functools.partial(merge_body, cfg), out_shape=tuple(out), in_specs=[VMEM] * 4, out_specs=(VMEM,) * 4, name="merge",
                          cost_estimate=pl.CostEstimate(flops=1 << 20, bytes_accessed=8 << 20, transcendentals=0))(*parts)


def split_body(cfg, query, key, value, d_attended, *outs):
    w, wide = cfg.width, cfg.heads * cfg.width
    core = lax.axis_index("inner") & 1
    for k, (pair, rows) in enumerate((outs[:2], outs[2:])):
        at = core ^ k
        pair[:, :w] = key[at]
        pair[:, w:] = value[at]
        rows[:, :wide] = query[at]
        rows[:, wide:] = d_attended[at]


def split(cfg, query, key, value, d_attended):
    n = cfg.tokens // 2
    out = [jax.ShapeDtypeStruct((n, 2 * cfg.width), bf16), jax.ShapeDtypeStruct((n, 2 * cfg.heads * cfg.width), bf16)] * 2
    return pl.pallas_call(functools.partial(split_body, cfg), out_shape=tuple(out), in_specs=[VMEM] * 4, out_specs=(VMEM,) * 4,
                          name="split")(query, key, value, d_attended)


def add(parts):
    return functools.reduce(jnp.add, [p.astype(f32) for p in parts])


def along_x(parts):
    return [parts[0]] + [shift(parts[d], dx=d) for d in range(1, NX)]


def gather(b, rows, made):
    n = b.shape[0]
    plus, minus = shift(b, dz=-2), shift(b, dz=2)
    right, left = shift(rows, dx=-1), shift(rows, dx=1)
    plus, minus, right, left, made = lax.optimization_barrier((plus, minus, right, left, made))
    up = shift(jnp.concatenate([b, plus], axis=0), dz=-1)
    down = shift(jnp.concatenate([b, minus], axis=0), dz=1)
    far = shift(plus, dz=-2)
    facing = shift(rows, dx=2)
    slab = jnp.concatenate([b, up[:n], plus, up[n:], far, down[n:], minus, down[:n]], axis=0)
    slab, facing = lax.optimization_barrier((slab, facing))
    return slab, [rows, right, facing, left], made


def scatter(slab, gq, n):
    at = [slab[d * n:(d + 1) * n] for d in range(NZ)]
    low = [v.astype(bf16) for v in at]
    up = shift(jnp.concatenate([low[1], low[3]], axis=0), dz=1)
    down = shift(jnp.concatenate([low[7], low[5]], axis=0), dz=-1)
    gq = along_x(gq)
    up, down, gq = lax.optimization_barrier((up, down, gq))
    far = shift(low[4], dz=4)
    plus = shift((at[2] + up[n:]).astype(bf16), dz=2)
    minus = shift((at[6] + down[n:]).astype(bf16), dz=-2)
    return add([at[0], up[:n], down[:n], far, plus, minus]), gq


def on_device(query, key, value, d_attended, stretch_ids):
    width = key.shape[2]
    cfg = Cfg(query.shape[2] // width, key.shape[1] // 2, width)
    core = lax.axis_index("inner") & 1
    sets = ((0,), (1,), (2,), (3,), (1, 3))
    pair, rows, pair_given, rows_given = split(cfg, query, key, value, d_attended)
    pair = jnp.concatenate([pair, shift(pair_given, core=1)], axis=0)
    rows = jnp.concatenate([rows, shift(rows_given, core=1)], axis=0)
    pair, rows = lax.optimization_barrier((pair, rows))
    slab, q, (tabs, qpos) = gather(pair, rows, tables(cfg, sets, stretch_ids))
    tab_near, tab_after, tab_across, tab_before, tab_beside = tabs
    after, before = shift(slab, dy=-1), shift(slab, dy=1)
    half = slab.shape[0] // 2
    qs, dos, *state = forward(cfg, tab_near, qpos, q, [slab], False)
    q = (qs, dos)
    opposite = jnp.concatenate([shift(before[:half], dy=1), shift(after[half:], dy=-1)], axis=0)
    state = forward(cfg, tab_beside, qpos, q, [after, before], False, state)
    stat, acc = forward(cfg, tab_across, qpos, q, [opposite], True, state)
    sent = parts(cfg, tab_near, stat, acc)
    stats = [stat] + [shift(stat, dx=-d) for d in range(1, NX)]
    stats, sent = lax.optimization_barrier((stats, sent))
    stat, gqt, gkv_across = backward(cfg, tab_across, qpos, q, [opposite], stats)
    first, second = shift(gkv_across[:half], dy=1), shift(gkv_across[half:], dy=-1)
    gqt, gkv_after = backward(cfg, tab_after, qpos, q, [after], [stat], gqt)
    gqt, first, second = lax.optimization_barrier((gqt, first, second))
    gqt, gkv_before = backward(cfg, tab_before, qpos, q, [before], [stat], gqt)
    gkv_after = jnp.concatenate([add([gkv_after[:half], first]).astype(bf16), gkv_after[half:]], axis=0)
    gkv_before = jnp.concatenate([gkv_before[:half], add([gkv_before[half:], second]).astype(bf16)], axis=0)
    got = [shift(gkv_after, dy=1), shift(gkv_before, dy=-1)]
    gq, gkv_near = backward(cfg, tab_near, qpos, q, [slab], [stat], gqt, sent)
    n = cfg.tokens
    gkv = add([gkv_near] + got)
    gkv, gq = lax.optimization_barrier((gkv, gq))
    gkv, gq = scatter(gkv, gq, n)
    att, att_given, gq, gq_given = merge(cfg, gq)

    def settled(mine, given):
        other = shift(given, core=1)
        return jnp.where(core == 0, jnp.stack([mine, other]), jnp.stack([other, mine]))

    att = settled(att, att_given)
    gq = settled(gq, gq_given)
    gkv = settled(gkv[:n // 2], gkv[n // 2:])
    return att, gq, gkv[..., :width] * width ** -0.5, gkv[..., width:]


def solution(mesh):
    split = P(None, AXES, None)
    return jax.shard_map(on_device, mesh=mesh, in_specs=(split,) * 4 + (P(),), out_specs=(split,) * 4, check_vma=False)
```

```python
import functools, math
import jax
import jax.numpy as jnp
from jax import lax
from jax.experimental import pallas as pl
from jax.experimental.pallas import tpu as pltpu
from jax.sharding import PartitionSpec as P

bf16, f32, i32 = jnp.bfloat16, jnp.float32, jnp.int32
HIDE = -float(2**18)
NONE = -1e30
NT = (((1,), (1,)), ((), ()))
NN = (((1,), (0,)), ((), ()))
SMEM = pl.BlockSpec(memory_space=pltpu.SMEM)
VMEM = pl.BlockSpec(memory_space=pltpu.VMEM)
LIMIT = 20 * 2**20
AXES = ("outer", "inner")
NX, NY, NZ = 4, 4, 8


def dot(a, b, dims=NN):
    return lax.dot_general(a, b, dims, preferred_element_type=f32)


class Cfg:
    def __init__(s, heads, half, width, C=256, R=256):
        s.heads, s.half, s.width, s.C, s.R = heads, half, width, C, R
        s.tokens = 4 * half
        s.span = half * heads
        s.row_blocks, s.slab_blocks = 4 * NX, 4 * NZ
        s.rows, s.slab = s.row_blocks * s.span, s.slab_blocks * half
        s.nr = s.rows // R


def place(x, y, z, core):
    return (x * 2 + (y >> 1)) * 32 + ((y & 1) * NZ + z) * 2 + core


def shift(a, dx=0, dy=0, dz=0, core=0):
    pairs = [(place(x, y, z, c), place((x + dx) % NX, (y + dy) % NY, (z + dz) % NZ, c ^ core))
             for x in range(NX) for y in range(NY) for z in range(NZ) for c in range(2)]
    return lax.ppermute(a, AXES, pairs)


def tables_body(cfg, sets, shard_count, ids, *refs):
    tabs, qpos_ref = refs[:-1], refs[-1]
    hf, span = cfg.half, cfg.span
    outer_at, inner_at = lax.axis_index("outer"), lax.axis_index("inner")
    x, core = outer_at >> 1, inner_at & 1
    y, z = (outer_at & 1) * 2 + (inner_at >> 4), (inner_at >> 1) & 7
    top = 2 * shard_count - 1
    line = lax.broadcasted_iota(i32, (1, 128), 1)

    def ranked(count, source):
        held = jnp.full((1, 128), 0, i32)
        for j in range(count):
            held = jnp.where(line >> 1 == j, ids[source(j)], held)
        held = jnp.where(line & 1 == 1, top - held, held)
        held = jnp.where(line < 2 * count, held, top + 1 + line).astype(f32)
        across = jnp.broadcast_to(held, (128, 128))
        down = across.T
        lane = lax.broadcasted_iota(i32, (128, 128), 1)
        rank = jnp.sum((down < across).astype(f32), axis=0, keepdims=True)
        rank_down = jnp.sum((across < down).astype(f32), axis=1, keepdims=True).astype(i32)
        rising = jnp.sum(jnp.where(rank_down == lane, down, 0.0), axis=0, keepdims=True)
        return rank, rising

    row_rank, rows = ranked(2 * NX, lambda j: place((x + (j >> 1)) & (NX - 1), y, z, core ^ (j & 1)))
    row_down = jnp.broadcast_to(rows, (128, 128)).T
    for slabs, tab_ref in zip(sets, tabs):
        key_rank, keys = ranked(
            2 * NZ * len(slabs), lambda j: place(x, (y + slabs[j >> 4]) & (NY - 1), (z + ((j >> 1) & 7)) & (NZ - 1), core ^ (j & 1)))
        counts = jnp.zeros((1, 128), f32)
        for r in range(cfg.nr):
            last = ((r + 1) * cfg.R - 1) // span
            seen = jnp.sum((keys <= row_down[last:last + 1]).astype(f32), axis=1, keepdims=True)
            chunks = jnp.maximum(jnp.floor((seen * hf + (cfg.C - 1)) * (1.0 / cfg.C)), 1.0)
            counts = jnp.where(line == r, chunks, counts) + jnp.where(line == 127, chunks, 0.0)
        tab_ref[0:1] = row_rank.astype(i32)
        tab_ref[1:2] = key_rank.astype(i32)
        tab_ref[2:3] = keys.astype(i32)
        tab_ref[3:4] = counts.astype(i32)
    spot = lax.broadcasted_iota(i32, (1, cfg.rows), 1)
    pos = jnp.zeros((1, cfg.rows), f32)
    for i in range(cfg.row_blocks):
        pos = jnp.where(spot >= i * span, row_down[i:i + 1, :1], pos)
    qpos_ref[...] = pos.astype(i32) * hf + (spot & (hf - 1))


def tables(cfg, sets, ids):
    found = pl.pallas_call(
        functools.partial(tables_body, cfg, sets, ids.shape[0]),
        out_shape=(jax.ShapeDtypeStruct((4, 128), i32),) * len(sets) + (jax.ShapeDtypeStruct((1, cfg.rows), i32),),
        in_specs=[SMEM], out_specs=(VMEM,) * (len(sets) + 1), name="tables",
        compiler_params=pltpu.CompilerParams(vmem_limit_bytes=4 * 2**20),
    )(ids)
    return found[:-1], found[-1]


def aligned(at, by):
    return at * by if isinstance(at, int) else pl.multiple_of(at * by, by)


def load_rows(cfg, tab, sources, dst, base=0):
    w, hf, hd = cfg.width, cfg.half, cfg.heads
    for i in range(cfg.row_blocks):
        at = aligned(tab[0, i], cfg.span)
        for h in range(hd):
            dst[pl.ds(pl.multiple_of(at + h * hf, hf), hf), :] = sources[i // 4][(i % 4) * hf:(i % 4 + 1) * hf, (base + h) * w:(base + h + 1) * w]


def load_keys(cfg, tab, sources, ks, vs, kpos):
    w, hf = cfg.width, cfg.half
    offset = lax.broadcasted_iota(i32, (hf, 128), 0)
    for j in range(ks.shape[0] // hf):
        kpos[j * hf:(j + 1) * hf, :] = offset + tab[2, j] * hf
    per = cfg.slab_blocks
    for n, source in enumerate(sources):
        def step(j, _):
            to = pl.ds(aligned(tab[1, n * per + j], hf), hf)
            block = source[pl.ds(aligned(j, hf), hf), :]
            ks[to, :] = block[:, :w]
            vs[to, :] = block[:, w:]
            return 0

        lax.fori_loop(0, per, step, 0, unroll=4)


def unload_rows(cfg, tab, src, outs):
    w, hf, hd = cfg.width, cfg.half, cfg.heads
    for i in range(cfg.row_blocks):
        at = aligned(tab[0, i], cfg.span)
        for h in range(hd):
            outs[i // 4][(i % 4) * hf:(i % 4 + 1) * hf, h * w:(h + 1) * w] = src[pl.ds(pl.multiple_of(at + h * hf, hf), hf), :].astype(bf16)


def visible(cfg, kpos, qpos_ref, c, r):
    C, R = cfg.C, cfg.R
    wide = jnp.concatenate([kpos[pl.ds(aligned(c, C), C), :]] * (R // 128), axis=1)
    return wide <= qpos_ref[:, pl.ds(aligned(r, R), R)]


def each_tile(cfg, tab, nc, count, stages):
    def step(_, at):
        group = []
        for _ in range(count):
            r, c = at
            past = r >= cfg.nr
            group.append((jnp.where(past, 0, r), jnp.where(past, nc - 1, c)))
            end = c + 1 >= tab[3, jnp.where(past, 0, r)]
            at = (jnp.where(end, r + 1, r), jnp.where(end, 0, c + 1))
        held = [()] * count
        for stage in stages:
            held = [stage(*spot, *value) for spot, value in zip(group, held)]
        return at

    lax.fori_loop(0, lax.div(tab[3, 127] + (count - 1), count), step, (jnp.int32(0), jnp.int32(0)))


def work(cfg, n, products):
    pairs = cfg.rows * n * cfg.slab * 5 // 8
    return pl.CostEstimate(flops=4 * products * cfg.width * pairs, bytes_accessed=4 << 20, transcendentals=pairs)


def forward_body(cfg, n, first, last, *refs):
    refs = list(refs)
    take = lambda k: [refs.pop(0) for _ in range(k)]
    (tab, qpos), q, kv = take(2), take(4 if first else 2), take(n)
    before = [] if first else take(2)
    qs, dos = take(2) if first else q
    (stat_ref,) = take(1) if last else [None]
    ml, acc = take(2)
    ks, vs, vt, kpos = take(4)
    w, C, R = cfg.width, cfg.C, cfg.R
    keys = n * cfg.slab
    if first:
        load_rows(cfg, tab, q, qs)
        load_rows(cfg, tab, q, dos, cfg.heads)
    load_keys(cfg, tab, kv, ks, vs, kpos)
    for c in range(keys // 256):
        vt[:, c * 256:(c + 1) * 256] = vs[c * 256:(c + 1) * 256, :].T
    if first:
        ml[0:1, :] = jnp.full((1, cfg.rows), NONE, f32)
        ml[1:2, :] = jnp.zeros((1, cfg.rows), f32)
        acc[...] = jnp.zeros_like(acc)
    else:
        ml[...] = before[0][...]
        acc[...] = before[1][...]
    scale = math.log2(math.e) / math.sqrt(w)

    def scores(r, c):
        s = dot(ks[pl.ds(aligned(c, C), C), :], qs[pl.ds(aligned(r, R), R), :], NT)
        return (jnp.where(visible(cfg, kpos, qpos, c, r), s, HIDE),)

    def weights(r, c, s):
        top = jnp.max(s, axis=0, keepdims=True) * scale
        p = jnp.exp2(s * scale - top)
        return top, jnp.sum(p, axis=0, keepdims=True), dot(vt[:, pl.ds(aligned(c, C), C)], p.astype(bf16))

    def absorb(r, c, top, total, mixed):
        here = pl.ds(aligned(r, R), R)
        old = ml[0:1, here]
        new = jnp.maximum(old, top)
        kept, added = jnp.exp2(old - new), jnp.exp2(top - new)
        ml[0:1, here] = new
        ml[1:2, here] = ml[1:2, here] * kept + total * added
        acc[:, here] = acc[:, here] * kept + mixed * added
        return ()

    each_tile(cfg, tab, keys // C, 8, (scores, weights, absorb))
    if not last:
        return

    def settle(r, _):
        here = pl.ds(aligned(r, 256), 256)
        safe = jnp.maximum(ml[1:2, here], 1e-30)
        mixed = acc[:, here] * (1.0 / safe)
        acc[:, here] = mixed
        stat_ref[0:1, here] = ml[0:1, here] + jnp.log2(safe)
        stat_ref[1:2, here] = jnp.sum(mixed * dos[here, :].astype(f32).T, axis=0, keepdims=True)
        return 0

    lax.fori_loop(0, cfg.rows // 256, settle, 0, unroll=2)


def parts_body(cfg, tab, stat_ref, acc, *refs):
    outs, (os, ls) = refs[:4], refs[4:]
    w, hf, hd = cfg.width, cfg.half, cfg.heads

    def turn(r, _):
        here = pl.ds(aligned(r, 256), 256)
        os[here, :] = acc[:, here].T
        ls[here, :] = jnp.broadcast_to(stat_ref[0:1, here], (w, 256)).T
        return 0

    lax.fori_loop(0, cfg.rows // 256, turn, 0, unroll=2)
    unload_rows(cfg, tab, os, outs)
    lane = lax.broadcasted_iota(i32, (hf, w), 1)
    for i in range(cfg.row_blocks):
        at = aligned(tab[0, i], cfg.span)
        extra = jnp.zeros((hf, w), f32)
        for h in range(hd):
            rest = ls[pl.ds(pl.multiple_of(at + h * hf, hf), hf), :]
            for k in range(3):
                piece = rest.astype(bf16).astype(f32)
                extra = jnp.where(lane == 3 * h + k, piece, extra)
                rest = rest - piece
        outs[i // 4][(i % 4) * hf:(i % 4 + 1) * hf, hd * w:] = extra.astype(bf16)


def parts(cfg, tab, stat, acc):
    row = (cfg.rows, cfg.width)
    return pl.pallas_call(
        functools.partial(parts_body, cfg), out_shape=(jax.ShapeDtypeStruct((cfg.tokens, (cfg.heads + 1) * cfg.width), bf16),) * 4,
        in_specs=[SMEM, VMEM, VMEM], out_specs=(VMEM,) * 4, scratch_shapes=[pltpu.VMEM(row, f32)] * 2, name="parts",
        compiler_params=pltpu.CompilerParams(vmem_limit_bytes=12 * 2**20),
        cost_estimate=pl.CostEstimate(flops=1 << 20, bytes_accessed=12 << 20, transcendentals=0),
    )(tab, stat, acc)


def forward(cfg, tab, qpos, q, kv, last, before=None):
    first, n, w = before is None, len(kv), cfg.width
    row, key = (cfg.rows, w), (n * cfg.slab, w)
    state = [jax.ShapeDtypeStruct((2, cfg.rows), f32), jax.ShapeDtypeStruct((w, cfg.rows), f32)]
    out = ([jax.ShapeDtypeStruct(row, bf16)] * 2 if first else []) + ([state[0]] if last else []) + state
    scratch = [pltpu.VMEM(key, bf16), pltpu.VMEM(key, bf16), pltpu.VMEM(key[::-1], bf16), pltpu.VMEM((key[0], 128), i32)]
    given = [tab, qpos, *q, *kv, *(before or ())]
    found = pl.pallas_call(
        functools.partial(forward_body, cfg, n, first, last), out_shape=tuple(out),
        in_specs=[SMEM] + [VMEM] * (len(given) - 1), out_specs=(VMEM,) * len(out), scratch_shapes=scratch,
        compiler_params=pltpu.CompilerParams(vmem_limit_bytes=LIMIT), name="attend", cost_estimate=work(cfg, n, 2),
    )(*given)
    return (found[0], found[2]) if last else found


def backward_body(cfg, n, first, last, *refs):
    refs = list(refs)
    take = lambda k: [refs.pop(0) for _ in range(k)]
    (tab, qpos, qs, dos), kv, stat = take(4), take(n), take(4 if first else 1)
    before = [] if first else take(1)
    parts_in = take(4) if last else []
    gq = take(4) if last else []
    (ld,) = take(1) if first else stat
    gqt = [] if last else take(1)
    gkv = take(n)
    ks, vs, kt, gks, gvs, kpos = take(6)
    gqt, gqs = (take(2) if last else (gqt[0], None))
    w, C, R, hf = cfg.width, cfg.C, cfg.R, cfg.half
    keys = n * cfg.slab
    load_keys(cfg, tab, kv, ks, vs, kpos)
    for c in range(keys // 256):
        kt[:, c * 256:(c + 1) * 256] = ks[c * 256:(c + 1) * 256, :].T
    gks[...] = jnp.zeros_like(gks)
    gvs[...] = jnp.zeros_like(gvs)
    gqt[...] = jnp.zeros_like(gqt) if first else before[0][...]
    if first:
        part = [s[0:1, :] for s in stat]
        top = functools.reduce(jnp.maximum, part)
        share = [jnp.exp2(v - top) for v in part]
        total = sum(share)
        ld[0:1, :] = top + jnp.log2(total)
        ld[1:2, :] = sum(v * s[1:2, :] for v, s in zip(share, stat)) / total
    scale = math.log2(math.e) / math.sqrt(w)

    def scores(r, c):
        at, here = pl.ds(aligned(c, C), C), pl.ds(aligned(r, R), R)
        s = dot(ks[at, :], qs[here, :], NT)
        gw = dot(vs[at, :], dos[here, :], NT)
        return jnp.where(visible(cfg, kpos, qpos, c, r), s, HIDE), gw

    def weights(r, c, s, gw):
        here = pl.ds(aligned(r, R), R)
        p = jnp.exp2(s * scale - ld[0:1, here])
        return p.astype(bf16), (p * (gw - ld[1:2, here])).astype(bf16)

    def products(r, c, p, ds):
        at, here = pl.ds(aligned(c, C), C), pl.ds(aligned(r, R), R)
        return dot(p, dos[here, :]), dot(ds, qs[here, :]), dot(kt[:, at], ds)

    def absorb(r, c, gv, gk, gq):
        at, here = pl.ds(aligned(c, C), C), pl.ds(aligned(r, R), R)
        gvs[at, :] += gv
        gks[at, :] += gk
        gqt[:, here] += gq
        return ()

    each_tile(cfg, tab, keys // C, 4, (scores, weights, products, absorb))
    if last:
        def turn(r, _):
            here = pl.ds(aligned(r, 256), 256)
            gqs[here, :] = gqt[:, here].T
            return 0

        lax.fori_loop(0, cfg.rows // 256, turn, 0, unroll=2)
        unload_rows(cfg, tab, gqs, gq)
        for part, out in zip(parts_in, gq):
            out[:, cfg.heads * w:] = part[...]
    for k, out in enumerate(gkv):
        def put(j, _):
            own = pl.ds(aligned(tab[1, k * cfg.slab_blocks + j], hf), hf)
            to = pl.ds(aligned(j, hf), hf)
            out[to, :w] = gks[own, :].astype(bf16)
            out[to, w:] = gvs[own, :].astype(bf16)
            return 0

        lax.fori_loop(0, cfg.slab_blocks, put, 0, unroll=4)


def backward(cfg, tab, qpos, q, kv, stat, before=None, parts=None):
    first, last, n, w = before is None, parts is not None, len(kv), cfg.width
    row, key = (cfg.rows, w), (n * cfg.slab, w)
    if last:
        out = [jax.ShapeDtypeStruct((cfg.tokens, (2 * cfg.heads + 1) * w), bf16)] * 4
    else:
        out = ([jax.ShapeDtypeStruct((2, cfg.rows), f32)] if first else []) + [jax.ShapeDtypeStruct(row[::-1], f32)]
    out += [jax.ShapeDtypeStruct((cfg.slab, 2 * w), bf16)] * n
    scratch = [pltpu.VMEM(key, bf16), pltpu.VMEM(key, bf16), pltpu.VMEM(key[::-1], bf16), pltpu.VMEM(key, f32), pltpu.VMEM(key, f32),
               pltpu.VMEM((key[0], 128), i32)]
    if last:
        scratch += [pltpu.VMEM(row[::-1], f32), pltpu.VMEM(row, f32)]
    given = [tab, qpos, *q, *kv, *stat] + ([] if first else [before]) + list(parts or ())
    found = pl.pallas_call(
        functools.partial(backward_body, cfg, n, first, last), out_shape=tuple(out),
        in_specs=[SMEM] + [VMEM] * (len(given) - 1), out_specs=(VMEM,) * len(out), scratch_shapes=scratch,
        compiler_params=pltpu.CompilerParams(vmem_limit_bytes=LIMIT), name="grads", cost_estimate=work(cfg, n, 5),
    )(*given)
    return (found[:4], found[4]) if last else found


def merge_body(cfg, *refs):
    parts, outs = refs[:4], refs[4:]
    w, hd, n = cfg.width, cfg.heads, cfg.tokens // 2
    scaling = w ** -0.5
    extra = [p[:, 2 * hd * w:].astype(f32) for p in parts]
    level = [e + pltpu.roll(e, w - 1, 1) + pltpu.roll(e, w - 2, 1) for e in extra]
    top = functools.reduce(jnp.maximum, level)
    share = [jnp.exp2(v - top) for v in level]
    total = 1.0 / sum(share)
    share = [v * total for v in share]
    for h in range(hd):
        at, behind = slice(h * w, (h + 1) * w), slice((hd + h) * w, (hd + h + 1) * w)
        mixed = sum(p[:, behind].astype(f32) * v[:, 3 * h:3 * h + 1] for p, v in zip(parts, share)).astype(bf16)
        outs[0][:, at] = mixed[:n]
        outs[1][:, at] = mixed[n:]
        summed = sum(p[:, at].astype(f32) for p in parts) * scaling
        outs[2][:, at] = summed[:n]
        outs[3][:, at] = summed[n:]


def merge(cfg, parts):
    out = [jax.ShapeDtypeStruct((cfg.tokens // 2, cfg.heads * cfg.width), t) for t in (bf16, bf16, f32, f32)]
    return pl.pallas_call(functools.partial(merge_body, cfg), out_shape=tuple(out), in_specs=[VMEM] * 4, out_specs=(VMEM,) * 4, name="merge",
                          compiler_params=pltpu.CompilerParams(vmem_limit_bytes=8 * 2**20),
                          cost_estimate=pl.CostEstimate(flops=1 << 20, bytes_accessed=8 << 20, transcendentals=0))(*parts)


def split_body(cfg, query, key, value, d_attended, *outs):
    w, wide = cfg.width, cfg.heads * cfg.width
    core = lax.axis_index("inner") & 1
    for k, (pair, rows) in enumerate((outs[:2], outs[2:])):
        at = core ^ k
        pair[:, :w] = key[at]
        pair[:, w:] = value[at]
        rows[:, :wide] = query[at]
        rows[:, wide:] = d_attended[at]


def split(cfg, query, key, value, d_attended):
    n = cfg.tokens // 2
    out = [jax.ShapeDtypeStruct((n, 2 * cfg.width), bf16), jax.ShapeDtypeStruct((n, 2 * cfg.heads * cfg.width), bf16)] * 2
    return pl.pallas_call(functools.partial(split_body, cfg), out_shape=tuple(out), in_specs=[VMEM] * 4, out_specs=(VMEM,) * 4,
                          compiler_params=pltpu.CompilerParams(vmem_limit_bytes=4 * 2**20), name="split")(query, key, value, d_attended)


def add(parts):
    return functools.reduce(jnp.add, [p.astype(f32) for p in parts])


def along_x(parts):
    return [parts[0]] + [shift(parts[d], dx=d) for d in range(1, NX)]


def gather(b, rows, made):
    n = b.shape[0]
    plus, minus = shift(b, dz=-2), shift(b, dz=2)
    right, left = shift(rows, dx=-1), shift(rows, dx=1)
    plus, minus, right, left, made = lax.optimization_barrier((plus, minus, right, left, made))
    up = shift(jnp.concatenate([b, plus], axis=0), dz=-1)
    down = shift(jnp.concatenate([b, minus], axis=0), dz=1)
    far = shift(plus, dz=-2)
    facing = shift(rows, dx=2)
    slab = jnp.concatenate([b, up[:n], plus, up[n:], far, down[n:], minus, down[:n]], axis=0)
    slab, facing = lax.optimization_barrier((slab, facing))
    return slab, [rows, right, facing, left], made


def scatter(slab, gq, n):
    at = [slab[d * n:(d + 1) * n] for d in range(NZ)]
    low = [v.astype(bf16) for v in at]
    up = shift(jnp.concatenate([low[1], low[3]], axis=0), dz=1)
    down = shift(jnp.concatenate([low[7], low[5]], axis=0), dz=-1)
    gq = along_x(gq)
    up, down, gq = lax.optimization_barrier((up, down, gq))
    far = shift(low[4], dz=4)
    plus = shift((at[2] + up[n:]).astype(bf16), dz=2)
    minus = shift((at[6] + down[n:]).astype(bf16), dz=-2)
    return add([at[0], up[:n], down[:n], far, plus, minus]), gq


def settle_body(core_axis, *refs):
    att, gq, gkv, att_got, gq_got, gkv_got, out, out_q, out_k, out_v = refs
    core = lax.axis_index(core_axis) & 1
    w = out_k.shape[2]
    for at, sources in ((core, (att, gq, gkv)), (1 - core, (att_got, gq_got, gkv_got))):
        out[at] = sources[0][...]
        out_q[at] = sources[1][...]
        out_k[at] = sources[2][:, :w] * w ** -0.5
        out_v[at] = sources[2][:, w:]


def settle(cfg, mine, got):
    n, w = cfg.tokens // 2, cfg.width
    out = [jax.ShapeDtypeStruct((2, n, cfg.heads * w), bf16), jax.ShapeDtypeStruct((2, n, cfg.heads * w), f32)]
    out += [jax.ShapeDtypeStruct((2, n, w), f32)] * 2
    return pl.pallas_call(functools.partial(settle_body, "inner"), out_shape=tuple(out), in_specs=[VMEM] * 6, out_specs=(VMEM,) * 4,
                          compiler_params=pltpu.CompilerParams(vmem_limit_bytes=4 * 2**20), name="settle")(*mine, *got)


def on_device(query, key, value, d_attended, stretch_ids):
    width = key.shape[2]
    cfg = Cfg(query.shape[2] // width, key.shape[1] // 2, width)
    sets = ((0,), (1,), (2,), (3,), (1, 3))
    pair, rows, pair_given, rows_given = split(cfg, query, key, value, d_attended)
    pair = jnp.concatenate([pair, shift(pair_given, core=1)], axis=0)
    rows = jnp.concatenate([rows, shift(rows_given, core=1)], axis=0)
    pair, rows = lax.optimization_barrier((pair, rows))
    slab, q, (tabs, qpos) = gather(pair, rows, tables(cfg, sets, stretch_ids))
    tab_near, tab_after, tab_across, tab_before, tab_beside = tabs
    after, before = shift(slab, dy=-1), shift(slab, dy=1)
    half = slab.shape[0] // 2
    qs, dos, *state = forward(cfg, tab_near, qpos, q, [slab], False)
    q = (qs, dos)
    opposite = jnp.concatenate([shift(before[:half], dy=1), shift(after[half:], dy=-1)], axis=0)
    state = forward(cfg, tab_beside, qpos, q, [after, before], False, state)
    stat, acc = forward(cfg, tab_across, qpos, q, [opposite], True, state)
    sent = parts(cfg, tab_near, stat, acc)
    stats = [stat] + [shift(stat, dx=-d) for d in range(1, NX)]
    stats, sent = lax.optimization_barrier((stats, sent))
    stat, gqt, gkv_across = backward(cfg, tab_across, qpos, q, [opposite], stats)
    first, second = shift(gkv_across[:half], dy=1), shift(gkv_across[half:], dy=-1)
    gqt, gkv_after = backward(cfg, tab_after, qpos, q, [after], [stat], gqt)
    gqt, first, second = lax.optimization_barrier((gqt, first, second))
    gqt, gkv_before = backward(cfg, tab_before, qpos, q, [before], [stat], gqt)
    gkv_after = jnp.concatenate([add([gkv_after[:half], first]).astype(bf16), gkv_after[half:]], axis=0)
    gkv_before = jnp.concatenate([gkv_before[:half], add([gkv_before[half:], second]).astype(bf16)], axis=0)
    got = [shift(gkv_after, dy=1), shift(gkv_before, dy=-1)]
    gq, gkv_near = backward(cfg, tab_near, qpos, q, [slab], [stat], gqt, sent)
    n = cfg.tokens
    gkv = add([gkv_near] + got)
    gkv, gq = lax.optimization_barrier((gkv, gq))
    gkv, gq = scatter(gkv, gq, n)
    att, att_given, gq, gq_given = merge(cfg, gq)

    given = [shift(v, core=1) for v in (att_given, gq_given, gkv[n // 2:])]
    return settle(cfg, [att, gq, gkv[:n // 2]], given)


def solution(mesh):
    split = P(None, AXES, None)
    return jax.shard_map(on_device, mesh=mesh, in_specs=(split,) * 4 + (P(),), out_specs=(split,) * 4, check_vma=False)
```

```python
import functools, math
import jax
import jax.numpy as jnp
from jax import lax
from jax.experimental import pallas as pl
from jax.experimental.pallas import tpu as pltpu
from jax.sharding import PartitionSpec as P

bf16, f32, i32 = jnp.bfloat16, jnp.float32, jnp.int32
HIDE = -float(2**18)
NONE = -1e30
NT = (((1,), (1,)), ((), ()))
NN = (((1,), (0,)), ((), ()))
SMEM = pl.BlockSpec(memory_space=pltpu.SMEM)
VMEM = pl.BlockSpec(memory_space=pltpu.VMEM)
LIMIT = 20 * 2**20
AXES = ("outer", "inner")
NX, NY, NZ = 4, 4, 8


def dot(a, b, dims=NN):
    return lax.dot_general(a, b, dims, preferred_element_type=f32)


class Cfg:
    def __init__(s, heads, half, width, C=256, R=256):
        s.heads, s.half, s.width, s.C, s.R = heads, half, width, C, R
        s.tokens = 4 * half
        s.span = half * heads
        s.row_blocks, s.slab_blocks = 4 * NX, 4 * NZ
        s.rows, s.slab = s.row_blocks * s.span, s.slab_blocks * half
        s.nr = s.rows // R


def place(x, y, z, core):
    return (x * 2 + (y >> 1)) * 32 + ((y & 1) * NZ + z) * 2 + core


def shift(a, dx=0, dy=0, dz=0, core=0):
    pairs = [(place(x, y, z, c), place((x + dx) % NX, (y + dy) % NY, (z + dz) % NZ, c ^ core))
             for x in range(NX) for y in range(NY) for z in range(NZ) for c in range(2)]
    return lax.ppermute(a, AXES, pairs)


def tables_body(cfg, sets, shard_count, ids, *refs):
    tabs, qpos_ref = refs[:-1], refs[-1]
    hf, span = cfg.half, cfg.span
    outer_at, inner_at = lax.axis_index("outer"), lax.axis_index("inner")
    x, core = outer_at >> 1, inner_at & 1
    y, z = (outer_at & 1) * 2 + (inner_at >> 4), (inner_at >> 1) & 7
    top = 2 * shard_count - 1
    line = lax.broadcasted_iota(i32, (1, 128), 1)

    def ranked(count, source):
        held = jnp.full((1, 128), 0, i32)
        for j in range(count):
            held = jnp.where(line >> 1 == j, ids[source(j)], held)
        held = jnp.where(line & 1 == 1, top - held, held)
        held = jnp.where(line < 2 * count, held, top + 1 + line).astype(f32)
        across = jnp.broadcast_to(held, (128, 128))
        down = across.T
        lane = lax.broadcasted_iota(i32, (128, 128), 1)
        rank = jnp.sum((down < across).astype(f32), axis=0, keepdims=True)
        rank_down = jnp.sum((across < down).astype(f32), axis=1, keepdims=True).astype(i32)
        rising = jnp.sum(jnp.where(rank_down == lane, down, 0.0), axis=0, keepdims=True)
        return rank, rising

    row_rank, rows = ranked(2 * NX, lambda j: place((x + (j >> 1)) & (NX - 1), y, z, core ^ (j & 1)))
    row_down = jnp.broadcast_to(rows, (128, 128)).T
    for slabs, tab_ref in zip(sets, tabs):
        key_rank, keys = ranked(
            2 * NZ * len(slabs), lambda j: place(x, (y + slabs[j >> 4]) & (NY - 1), (z + ((j >> 1) & 7)) & (NZ - 1), core ^ (j & 1)))
        counts = jnp.zeros((1, 128), f32)
        for r in range(cfg.nr):
            last = ((r + 1) * cfg.R - 1) // span
            seen = jnp.sum((keys <= row_down[last:last + 1]).astype(f32), axis=1, keepdims=True)
            chunks = jnp.maximum(jnp.floor((seen * hf + (cfg.C - 1)) * (1.0 / cfg.C)), 1.0)
            counts = jnp.where(line == r, chunks, counts) + jnp.where(line == 127, chunks, 0.0)
        tab_ref[0:1] = row_rank.astype(i32)
        tab_ref[1:2] = key_rank.astype(i32)
        tab_ref[2:3] = keys.astype(i32)
        tab_ref[3:4] = counts.astype(i32)
    spot = lax.broadcasted_iota(i32, (1, cfg.rows), 1)
    pos = jnp.zeros((1, cfg.rows), f32)
    for i in range(cfg.row_blocks):
        pos = jnp.where(spot >= i * span, row_down[i:i + 1, :1], pos)
    qpos_ref[...] = pos.astype(i32) * hf + (spot & (hf - 1))


def tables(cfg, sets, ids):
    found = pl.pallas_call(
        functools.partial(tables_body, cfg, sets, ids.shape[0]),
        out_shape=(jax.ShapeDtypeStruct((4, 128), i32),) * len(sets) + (jax.ShapeDtypeStruct((1, cfg.rows), i32),),
        in_specs=[SMEM], out_specs=(VMEM,) * (len(sets) + 1), name="tables",
        compiler_params=pltpu.CompilerParams(vmem_limit_bytes=4 * 2**20),
    )(ids)
    return found[:-1], found[-1]


def aligned(at, by):
    return at * by if isinstance(at, int) else pl.multiple_of(at * by, by)


def load_rows(cfg, tab, sources, dst, base=0):
    w, hf, hd = cfg.width, cfg.half, cfg.heads
    for i in range(cfg.row_blocks):
        at = aligned(tab[0, i], cfg.span)
        for h in range(hd):
            dst[pl.ds(pl.multiple_of(at + h * hf, hf), hf), :] = sources[i // 4][(i % 4) * hf:(i % 4 + 1) * hf, (base + h) * w:(base + h + 1) * w]


def load_keys(cfg, tab, sources, ks, vs, kpos):
    w, hf = cfg.width, cfg.half
    offset = lax.broadcasted_iota(i32, (hf, 128), 0)
    for j in range(ks.shape[0] // hf):
        kpos[j * hf:(j + 1) * hf, :] = offset + tab[2, j] * hf
    per = cfg.slab_blocks
    for n, source in enumerate(sources):
        def step(j, _):
            to = pl.ds(aligned(tab[1, n * per + j], hf), hf)
            block = source[pl.ds(aligned(j, hf), hf), :]
            ks[to, :] = block[:, :w]
            vs[to, :] = block[:, w:]
            return 0

        lax.fori_loop(0, per, step, 0, unroll=4)


def unload_rows(cfg, tab, src, outs):
    w, hf, hd = cfg.width, cfg.half, cfg.heads
    for i in range(cfg.row_blocks):
        at = aligned(tab[0, i], cfg.span)
        for h in range(hd):
            outs[i // 4][(i % 4) * hf:(i % 4 + 1) * hf, h * w:(h + 1) * w] = src[pl.ds(pl.multiple_of(at + h * hf, hf), hf), :].astype(bf16)


def visible(cfg, kpos, qpos_ref, c, r):
    C, R = cfg.C, cfg.R
    wide = jnp.concatenate([kpos[pl.ds(aligned(c, C), C), :]] * (R // 128), axis=1)
    return wide <= qpos_ref[:, pl.ds(aligned(r, R), R)]


def each_tile(cfg, tab, nc, count, stages):
    def step(_, at):
        group = []
        for _ in range(count):
            r, c = at
            past = r >= cfg.nr
            group.append((jnp.where(past, 0, r), jnp.where(past, nc - 1, c)))
            end = c + 1 >= tab[3, jnp.where(past, 0, r)]
            at = (jnp.where(end, r + 1, r), jnp.where(end, 0, c + 1))
        held = [()] * count
        for stage in stages:
            held = [stage(*spot, *value) for spot, value in zip(group, held)]
        return at

    lax.fori_loop(0, lax.div(tab[3, 127] + (count - 1), count), step, (jnp.int32(0), jnp.int32(0)))


def work(cfg, n, products):
    pairs = cfg.rows * n * cfg.slab * 5 // 8
    return pl.CostEstimate(flops=4 * products * cfg.width * pairs, bytes_accessed=4 << 20, transcendentals=pairs)


def forward_body(cfg, n, first, last, *refs):
    refs = list(refs)
    take = lambda k: [refs.pop(0) for _ in range(k)]
    (tab, qpos), q, kv = take(2), take(4 if first else 2), take(n)
    before = [] if first else take(2)
    qs, dos = take(2) if first else q
    (stat_ref,) = take(1) if last else [None]
    ml, acc = take(2)
    ks, vs, vt, kpos = take(4)
    w, C, R = cfg.width, cfg.C, cfg.R
    keys = n * cfg.slab
    if first:
        load_rows(cfg, tab, q, qs)
        load_rows(cfg, tab, q, dos, cfg.heads)
    load_keys(cfg, tab, kv, ks, vs, kpos)
    for c in range(keys // 256):
        vt[:, c * 256:(c + 1) * 256] = vs[c * 256:(c + 1) * 256, :].T
    if first:
        ml[0:1, :] = jnp.full((1, cfg.rows), NONE, f32)
        ml[1:2, :] = jnp.zeros((1, cfg.rows), f32)
        acc[...] = jnp.zeros_like(acc)
    else:
        ml[...] = before[0][...]
        acc[...] = before[1][...]
    scale = math.log2(math.e) / math.sqrt(w)

    def scores(r, c):
        s = dot(ks[pl.ds(aligned(c, C), C), :], qs[pl.ds(aligned(r, R), R), :], NT)
        return (jnp.where(visible(cfg, kpos, qpos, c, r), s, HIDE),)

    def weights(r, c, s):
        top = jnp.max(s, axis=0, keepdims=True) * scale
        p = jnp.exp2(s * scale - top)
        return top, jnp.sum(p, axis=0, keepdims=True), dot(vt[:, pl.ds(aligned(c, C), C)], p.astype(bf16))

    def absorb(r, c, top, total, mixed):
        here = pl.ds(aligned(r, R), R)
        old = ml[0:1, here]
        new = jnp.maximum(old, top)
        kept, added = jnp.exp2(old - new), jnp.exp2(top - new)
        ml[0:1, here] = new
        ml[1:2, here] = ml[1:2, here] * kept + total * added
        acc[:, here] = acc[:, here] * kept + mixed * added
        return ()

    each_tile(cfg, tab, keys // C, 7, (scores, weights, absorb))
    if not last:
        return

    def settle(r, _):
        here = pl.ds(aligned(r, 256), 256)
        safe = jnp.maximum(ml[1:2, here], 1e-30)
        mixed = acc[:, here] * (1.0 / safe)
        acc[:, here] = mixed
        stat_ref[0:1, here] = ml[0:1, here] + jnp.log2(safe)
        stat_ref[1:2, here] = jnp.sum(mixed * dos[here, :].astype(f32).T, axis=0, keepdims=True)
        return 0

    lax.fori_loop(0, cfg.rows // 256, settle, 0, unroll=2)


def parts_body(cfg, tab, stat_ref, acc, *refs):
    outs, (os, ls) = refs[:4], refs[4:]
    w, hf, hd = cfg.width, cfg.half, cfg.heads

    def turn(r, _):
        here = pl.ds(aligned(r, 256), 256)
        os[here, :] = acc[:, here].T
        ls[here, :] = jnp.broadcast_to(stat_ref[0:1, here], (w, 256)).T
        return 0

    lax.fori_loop(0, cfg.rows // 256, turn, 0, unroll=2)
    unload_rows(cfg, tab, os, outs)
    lane = lax.broadcasted_iota(i32, (hf, w), 1)
    for i in range(cfg.row_blocks):
        at = aligned(tab[0, i], cfg.span)
        extra = jnp.zeros((hf, w), f32)
        for h in range(hd):
            rest = ls[pl.ds(pl.multiple_of(at + h * hf, hf), hf), :]
            for k in range(3):
                piece = rest.astype(bf16).astype(f32)
                extra = jnp.where(lane == 3 * h + k, piece, extra)
                rest = rest - piece
        outs[i // 4][(i % 4) * hf:(i % 4 + 1) * hf, hd * w:] = extra.astype(bf16)


def parts(cfg, tab, stat, acc):
    row = (cfg.rows, cfg.width)
    return pl.pallas_call(
        functools.partial(parts_body, cfg), out_shape=(jax.ShapeDtypeStruct((cfg.tokens, (cfg.heads + 1) * cfg.width), bf16),) * 4,
        in_specs=[SMEM, VMEM, VMEM], out_specs=(VMEM,) * 4, scratch_shapes=[pltpu.VMEM(row, f32)] * 2, name="parts",
        compiler_params=pltpu.CompilerParams(vmem_limit_bytes=12 * 2**20),
        cost_estimate=pl.CostEstimate(flops=1 << 20, bytes_accessed=12 << 20, transcendentals=0),
    )(tab, stat, acc)


def forward(cfg, tab, qpos, q, kv, last, before=None):
    first, n, w = before is None, len(kv), cfg.width
    row, key = (cfg.rows, w), (n * cfg.slab, w)
    state = [jax.ShapeDtypeStruct((2, cfg.rows), f32), jax.ShapeDtypeStruct((w, cfg.rows), f32)]
    out = ([jax.ShapeDtypeStruct(row, bf16)] * 2 if first else []) + ([state[0]] if last else []) + state
    scratch = [pltpu.VMEM(key, bf16), pltpu.VMEM(key, bf16), pltpu.VMEM(key[::-1], bf16), pltpu.VMEM((key[0], 128), i32)]
    given = [tab, qpos, *q, *kv, *(before or ())]
    found = pl.pallas_call(
        functools.partial(forward_body, cfg, n, first, last), out_shape=tuple(out),
        in_specs=[SMEM] + [VMEM] * (len(given) - 1), out_specs=(VMEM,) * len(out), scratch_shapes=scratch,
        compiler_params=pltpu.CompilerParams(vmem_limit_bytes=LIMIT), name="attend", cost_estimate=work(cfg, n, 2),
    )(*given)
    return (found[0], found[2]) if last else found


def backward_body(cfg, n, first, last, *refs):
    refs = list(refs)
    take = lambda k: [refs.pop(0) for _ in range(k)]
    (tab, qpos, qs, dos), kv, stat = take(4), take(n), take(4 if first else 1)
    before = [] if first else take(1)
    parts_in = take(4) if last else []
    gq = take(4) if last else []
    (ld,) = take(1) if first else stat
    gqt = [] if last else take(1)
    gkv = take(n)
    ks, vs, kt, gks, gvs, kpos = take(6)
    gqt, gqs = (take(2) if last else (gqt[0], None))
    w, C, R, hf = cfg.width, cfg.C, cfg.R, cfg.half
    keys = n * cfg.slab
    load_keys(cfg, tab, kv, ks, vs, kpos)
    for c in range(keys // 256):
        kt[:, c * 256:(c + 1) * 256] = ks[c * 256:(c + 1) * 256, :].T
    gks[...] = jnp.zeros_like(gks)
    gvs[...] = jnp.zeros_like(gvs)
    gqt[...] = jnp.zeros_like(gqt) if first else before[0][...]
    if first:
        part = [s[0:1, :] for s in stat]
        top = functools.reduce(jnp.maximum, part)
        share = [jnp.exp2(v - top) for v in part]
        total = sum(share)
        ld[0:1, :] = top + jnp.log2(total)
        ld[1:2, :] = sum(v * s[1:2, :] for v, s in zip(share, stat)) / total
    scale = math.log2(math.e) / math.sqrt(w)

    def scores(r, c):
        at, here = pl.ds(aligned(c, C), C), pl.ds(aligned(r, R), R)
        s = dot(ks[at, :], qs[here, :], NT)
        gw = dot(vs[at, :], dos[here, :], NT)
        return jnp.where(visible(cfg, kpos, qpos, c, r), s, HIDE), gw

    def weights(r, c, s, gw):
        here = pl.ds(aligned(r, R), R)
        p = jnp.exp2(s * scale - ld[0:1, here])
        return p.astype(bf16), (p * (gw - ld[1:2, here])).astype(bf16)

    def products(r, c, p, ds):
        at, here = pl.ds(aligned(c, C), C), pl.ds(aligned(r, R), R)
        return dot(p, dos[here, :]), dot(ds, qs[here, :]), dot(kt[:, at], ds)

    def absorb(r, c, gv, gk, gq):
        at, here = pl.ds(aligned(c, C), C), pl.ds(aligned(r, R), R)
        gvs[at, :] += gv
        gks[at, :] += gk
        gqt[:, here] += gq
        return ()

    each_tile(cfg, tab, keys // C, 7, (scores, weights, products, absorb))
    if last:
        def turn(r, _):
            here = pl.ds(aligned(r, 256), 256)
            gqs[here, :] = gqt[:, here].T
            return 0

        lax.fori_loop(0, cfg.rows // 256, turn, 0, unroll=2)
        unload_rows(cfg, tab, gqs, gq)
        for part, out in zip(parts_in, gq):
            out[:, cfg.heads * w:] = part[...]
    for k, out in enumerate(gkv):
        def put(j, _):
            own = pl.ds(aligned(tab[1, k * cfg.slab_blocks + j], hf), hf)
            to = pl.ds(aligned(j, hf), hf)
            out[to, :w] = gks[own, :].astype(bf16)
            out[to, w:] = gvs[own, :].astype(bf16)
            return 0

        lax.fori_loop(0, cfg.slab_blocks, put, 0, unroll=4)


def backward(cfg, tab, qpos, q, kv, stat, before=None, parts=None):
    first, last, n, w = before is None, parts is not None, len(kv), cfg.width
    row, key = (cfg.rows, w), (n * cfg.slab, w)
    if last:
        out = [jax.ShapeDtypeStruct((cfg.tokens, (2 * cfg.heads + 1) * w), bf16)] * 4
    else:
        out = ([jax.ShapeDtypeStruct((2, cfg.rows), f32)] if first else []) + [jax.ShapeDtypeStruct(row[::-1], f32)]
    out += [jax.ShapeDtypeStruct((cfg.slab, 2 * w), bf16)] * n
    scratch = [pltpu.VMEM(key, bf16), pltpu.VMEM(key, bf16), pltpu.VMEM(key[::-1], bf16), pltpu.VMEM(key, f32), pltpu.VMEM(key, f32),
               pltpu.VMEM((key[0], 128), i32)]
    if last:
        scratch += [pltpu.VMEM(row[::-1], f32), pltpu.VMEM(row, f32)]
    given = [tab, qpos, *q, *kv, *stat] + ([] if first else [before]) + list(parts or ())
    found = pl.pallas_call(
        functools.partial(backward_body, cfg, n, first, last), out_shape=tuple(out),
        in_specs=[SMEM] + [VMEM] * (len(given) - 1), out_specs=(VMEM,) * len(out), scratch_shapes=scratch,
        compiler_params=pltpu.CompilerParams(vmem_limit_bytes=LIMIT), name="grads", cost_estimate=work(cfg, n, 5),
    )(*given)
    return (found[:4], found[4]) if last else found


def merge_body(cfg, *refs):
    parts, outs = refs[:4], refs[4:]
    w, hd, n = cfg.width, cfg.heads, cfg.tokens // 2
    scaling = w ** -0.5
    extra = [p[:, 2 * hd * w:].astype(f32) for p in parts]
    level = [e + pltpu.roll(e, w - 1, 1) + pltpu.roll(e, w - 2, 1) for e in extra]
    top = functools.reduce(jnp.maximum, level)
    share = [jnp.exp2(v - top) for v in level]
    total = 1.0 / sum(share)
    share = [v * total for v in share]
    for h in range(hd):
        at, behind = slice(h * w, (h + 1) * w), slice((hd + h) * w, (hd + h + 1) * w)
        mixed = sum(p[:, behind].astype(f32) * v[:, 3 * h:3 * h + 1] for p, v in zip(parts, share)).astype(bf16)
        outs[0][:, at] = mixed[:n]
        outs[1][:, at] = mixed[n:]
        summed = sum(p[:, at].astype(f32) for p in parts) * scaling
        outs[2][:, at] = summed[:n]
        outs[3][:, at] = summed[n:]


def merge(cfg, parts):
    out = [jax.ShapeDtypeStruct((cfg.tokens // 2, cfg.heads * cfg.width), t) for t in (bf16, bf16, f32, f32)]
    return pl.pallas_call(functools.partial(merge_body, cfg), out_shape=tuple(out), in_specs=[VMEM] * 4, out_specs=(VMEM,) * 4, name="merge",
                          compiler_params=pltpu.CompilerParams(vmem_limit_bytes=8 * 2**20),
                          cost_estimate=pl.CostEstimate(flops=1 << 20, bytes_accessed=8 << 20, transcendentals=0))(*parts)


def split_body(cfg, query, key, value, d_attended, *outs):
    w, wide = cfg.width, cfg.heads * cfg.width
    core = lax.axis_index("inner") & 1
    for k, (pair, rows) in enumerate((outs[:2], outs[2:])):
        at = core ^ k
        pair[:, :w] = key[at]
        pair[:, w:] = value[at]
        rows[:, :wide] = query[at]
        rows[:, wide:] = d_attended[at]


def split(cfg, query, key, value, d_attended):
    n = cfg.tokens // 2
    out = [jax.ShapeDtypeStruct((n, 2 * cfg.width), bf16), jax.ShapeDtypeStruct((n, 2 * cfg.heads * cfg.width), bf16)] * 2
    return pl.pallas_call(functools.partial(split_body, cfg), out_shape=tuple(out), in_specs=[VMEM] * 4, out_specs=(VMEM,) * 4,
                          compiler_params=pltpu.CompilerParams(vmem_limit_bytes=4 * 2**20), name="split")(query, key, value, d_attended)


def add(parts):
    return functools.reduce(jnp.add, [p.astype(f32) for p in parts])


def along_x(parts):
    return [parts[0]] + [shift(parts[d], dx=d) for d in range(1, NX)]


def gather(b, rows, made):
    n = b.shape[0]
    plus, minus = shift(b, dz=-2), shift(b, dz=2)
    right, left = shift(rows, dx=-1), shift(rows, dx=1)
    plus, minus, right, left, made = lax.optimization_barrier((plus, minus, right, left, made))
    up = shift(jnp.concatenate([b, plus], axis=0), dz=-1)
    down = shift(jnp.concatenate([b, minus], axis=0), dz=1)
    far = shift(plus, dz=-2)
    facing = shift(rows, dx=2)
    slab = jnp.concatenate([b, up[:n], plus, up[n:], far, down[n:], minus, down[:n]], axis=0)
    slab, facing = lax.optimization_barrier((slab, facing))
    return slab, [rows, right, facing, left], made


def scatter(slab, gq, n):
    at = [slab[d * n:(d + 1) * n] for d in range(NZ)]
    low = [v.astype(bf16) for v in at]
    up = shift(jnp.concatenate([low[1], low[3]], axis=0), dz=1)
    down = shift(jnp.concatenate([low[7], low[5]], axis=0), dz=-1)
    gq = along_x(gq)
    up, down, gq = lax.optimization_barrier((up, down, gq))
    far = shift(low[4], dz=4)
    plus = shift((at[2] + up[n:]).astype(bf16), dz=2)
    minus = shift((at[6] + down[n:]).astype(bf16), dz=-2)
    return add([at[0], up[:n], down[:n], far, plus, minus]), gq


def settle_body(core_axis, *refs):
    att, gq, gkv, att_got, gq_got, gkv_got, out, out_q, out_k, out_v = refs
    core = lax.axis_index(core_axis) & 1
    w = out_k.shape[2]
    for at, sources in ((core, (att, gq, gkv)), (1 - core, (att_got, gq_got, gkv_got))):
        out[at] = sources[0][...]
        out_q[at] = sources[1][...]
        out_k[at] = sources[2][:, :w] * w ** -0.5
        out_v[at] = sources[2][:, w:]


def settle(cfg, mine, got):
    n, w = cfg.tokens // 2, cfg.width
    out = [jax.ShapeDtypeStruct((2, n, cfg.heads * w), bf16), jax.ShapeDtypeStruct((2, n, cfg.heads * w), f32)]
    out += [jax.ShapeDtypeStruct((2, n, w), f32)] * 2
    return pl.pallas_call(functools.partial(settle_body, "inner"), out_shape=tuple(out), in_specs=[VMEM] * 6, out_specs=(VMEM,) * 4,
                          compiler_params=pltpu.CompilerParams(vmem_limit_bytes=4 * 2**20), name="settle")(*mine, *got)


def on_device(query, key, value, d_attended, stretch_ids):
    width = key.shape[2]
    cfg = Cfg(query.shape[2] // width, key.shape[1] // 2, width)
    sets = ((0,), (1,), (2,), (3,), (1, 3))
    pair, rows, pair_given, rows_given = split(cfg, query, key, value, d_attended)
    pair = jnp.concatenate([pair, shift(pair_given, core=1)], axis=0)
    rows = jnp.concatenate([rows, shift(rows_given, core=1)], axis=0)
    pair, rows = lax.optimization_barrier((pair, rows))
    slab, q, (tabs, qpos) = gather(pair, rows, tables(cfg, sets, stretch_ids))
    tab_near, tab_after, tab_across, tab_before, tab_beside = tabs
    after, before = shift(slab, dy=-1), shift(slab, dy=1)
    half = slab.shape[0] // 2
    qs, dos, *state = forward(cfg, tab_near, qpos, q, [slab], False)
    q = (qs, dos)
    opposite = jnp.concatenate([shift(before[:half], dy=1), shift(after[half:], dy=-1)], axis=0)
    state = forward(cfg, tab_beside, qpos, q, [after, before], False, state)
    stat, acc = forward(cfg, tab_across, qpos, q, [opposite], True, state)
    sent = parts(cfg, tab_near, stat, acc)
    stats = [stat] + [shift(stat, dx=-d) for d in range(1, NX)]
    stats, sent = lax.optimization_barrier((stats, sent))
    stat, gqt, gkv_across = backward(cfg, tab_across, qpos, q, [opposite], stats)
    first, second = shift(gkv_across[:half], dy=1), shift(gkv_across[half:], dy=-1)
    gqt, gkv_after = backward(cfg, tab_after, qpos, q, [after], [stat], gqt)
    gqt, first, second = lax.optimization_barrier((gqt, first, second))
    gqt, gkv_before = backward(cfg, tab_before, qpos, q, [before], [stat], gqt)
    gkv_after = jnp.concatenate([add([gkv_after[:half], first]).astype(bf16), gkv_after[half:]], axis=0)
    gkv_before = jnp.concatenate([gkv_before[:half], add([gkv_before[half:], second]).astype(bf16)], axis=0)
    got = [shift(gkv_after, dy=1), shift(gkv_before, dy=-1)]
    gq, gkv_near = backward(cfg, tab_near, qpos, q, [slab], [stat], gqt, sent)
    n = cfg.tokens
    gkv = add([gkv_near] + got)
    gkv, gq = lax.optimization_barrier((gkv, gq))
    gkv, gq = scatter(gkv, gq, n)
    att, att_given, gq, gq_given = merge(cfg, gq)

    given = [shift(v, core=1) for v in (att_given, gq_given, gkv[n // 2:])]
    return settle(cfg, [att, gq, gkv[:n // 2]], given)


def solution(mesh):
    split = P(None, AXES, None)
    return jax.shard_map(on_device, mesh=mesh, in_specs=(split,) * 4 + (P(),), out_specs=(split,) * 4, check_vma=False)
```
